512 devices in a mesh: band: 32 (over z_hi, y, x), sector: 16 (over z_lo, core).
Axes of the slice: x: 4, y: 4, z: 16 (z_hi: 2, z_lo: 8; z = z_hi * 8 + z_lo), core: 2. Of those that a mesh axis runs over, the one named last changes fastest.
Arguments:
- feats: bfloat16 [96, 64, 2048], P(None, 'band', 'sector'), may hold values from -6 to 6
- counts: int32 [64, 2048], P('band', 'sector'), may hold values from 0 to 15
- occupancy: int32 [64, 16], P('band', 'sector'), may hold values from 0 to 1, as said below
- window_ids: int32 [2048, 64], P('sector', 'band'), may hold values from 0 to 3, never falling along the last dimension, each value on 1 to 32 neighbouring positions
- w_qkv: bfloat16 [288, 96], replicated, may hold values from -1.1 to 1.15
- w_out: bfloat16 [96, 96], replicated, may hold values from -0.625 to 0.625
- conv_weight: bfloat16 [27, 96, 96], replicated, may hold values from -0.125 to 0.125
- cotangent: bfloat16 [96, 64, 2048], P(None, 'band', 'sector'), may hold values from -6 to 6
Outputs:
- section_out: bfloat16 [96, 64, 2048], P(None, 'band', 'sector')
- grad_weight: float32 [27, 96, 96], replicated
- grad_mid: bfloat16 [96, 64, 2048], P(None, 'band', 'sector')
The draws below stay inside these ranges and needn't reach their ends.
Inputs may be any that keep to these rules, and one draw needn't show every extreme that they name: `window_ids`: window numbers never fall along a ray; each window holds 1 to 32 cells. `occupancy`: tiles near the sensor are occupied more often.
All inputs are finite; a program needn't handle non-finite values.
Results may differ from the reference program's by a relative error of at most 0.008.
Values may be sent and summed in bfloat16 or wider, within the bound.
No kernel may reach another device: no remote copies, remote signals or barrier semaphores. Data moves between devices by JAX's collectives and lax.ppermute only.
A program may use at most 64 MiB of HBM per device.

```python
import math
import jax
import jax.numpy as jnp
import numpy as np
from jax import lax

C = 96
HEAD_DIM = 16
HEADS = 6
INC = 32
RAD = 64
AZI = 64
CELLS = 2048
TILES = 16


def draw_occupancy(key, part):
    radius = jnp.arange(RAD, dtype=jnp.int32)[:, None]
    limit = 90 - 80 * radius // RAD
    drawn = jax.random.randint(key, (RAD, TILES), 0, 100)
    return (drawn < limit).astype(jnp.int32)


def draw_feats(key, part):
    noise = jax.random.normal(jax.random.fold_in(key, 11), (C, RAD, CELLS), jnp.float32)
    entries = jnp.clip(noise, -6.0, 6.0)
    return entries.astype(jnp.bfloat16)


def draw_w_qkv(key, part):
    noise = jax.random.normal(jax.random.fold_in(key, 21), (3 * C, C), jnp.float32)
    entries = jnp.clip(noise, -6.0, 6.0) * C ** (-0.5)
    return entries.astype(jnp.bfloat16)


def place_ends(values, rng, smallest, top_value):
    longest = values.shape.index(max(values.shape))
    spots = []
    for shift in (0, 1):
        where = [jax.random.randint(jax.random.fold_in(rng, axis), (), 0, length) for axis, length in enumerate(values.shape)]
        where[longest] = (where[longest] + shift) % values.shape[longest]
        spots.append(tuple(where))
    return values.at[spots[0]].set(smallest).at[spots[1]].set(top_value)


def levels(rng, dims, shards, smallest, largest):
    level = 1.0
    for axis_at, parts in shards:
        steps = jax.random.uniform(jax.random.fold_in(jax.random.fold_in(rng, 6), axis_at), (parts,), jnp.float32, smallest / len(shards), largest / len(shards))
        level = level * jnp.repeat(jnp.exp(steps), dims[axis_at] // parts).reshape((-1,) + (1,) * (len(dims) - 1 - axis_at))
    return level


def profile(number_of, total, bound, lean):
    portions = [(1 << 20) // math.isqrt(rank ** lean) + 1 for rank in range(2, number_of + 1)]
    spare, given = total - bound - (number_of - 1), [1] * (number_of - 1)
    while spare > 0:
        movable = [i for i in range(number_of - 1) if given[i] < bound]
        whole, budget = sum([portions[i] for i in movable]), spare
        for i in movable:
            extra = min(bound - given[i], max(1, budget * portions[i] // whole), spare)
            given[i] = given[i] + extra
            spare = spare - extra
    return np.array([bound] + given)


def uneven(key, amount, total, most, lean):
    if amount == 2:
        one = jax.random.randint(key, (), max(1, total - most), min(most, total - 1) + 1)
        return jnp.stack([one, total - one])
    lengths = jnp.asarray(profile(amount, total, most, lean), jnp.int32)
    twos = (amount - 1) // 2
    donor, sink = lengths[1:1 + 2 * twos:2], lengths[2:2 + 2 * twos:2]
    room = jnp.minimum(donor - 1, most - sink)
    moved = jax.random.randint(jax.random.fold_in(key, 1), (twos,), 0, 1 << 20) % (room + 1)
    lengths = lengths.at[1:1 + 2 * twos:2].set(donor - moved).at[2:2 + 2 * twos:2].set(sink + moved)
    return lengths[jax.random.permutation(jax.random.fold_in(key, 2), amount)]


def normal_values(rng, dims, deviation, most, cuts=(), kind=jnp.bfloat16):
    array = deviation * jax.random.normal(rng, dims, jnp.float32)
    if cuts:
        array = array * levels(rng, dims, cuts, -0.22, 0.18)
    return jnp.clip(array, -most, most).astype(kind)


def setup_inputs(seed: int = 0) -> dict:
    keys = jax.random.split(jax.random.key(seed), 9)
    return {
        "feats": draw_feats(jax.random.fold_in(keys[8], 71), 0),
        "counts": place_ends(jax.random.randint(keys[1], (RAD, CELLS), 0, 16), jax.random.fold_in(keys[1], 1), 0, 15).astype(jnp.int32),
        "occupancy": draw_occupancy(jax.random.fold_in(keys[8], 71), 0),
        "window_ids": jax.vmap(lambda own: jnp.searchsorted(jnp.cumsum(uneven(own, 4, RAD, RAD // 2, 0)), jnp.arange(RAD), side="right"))(jax.random.split(keys[3], CELLS)).reshape((CELLS, RAD)).astype(jnp.int32),
        "w_qkv": draw_w_qkv(jax.random.fold_in(keys[8], 71), 0),
        "w_out": normal_values(keys[5], (C, C), C ** -0.5, 0.625),
        "conv_weight": normal_values(keys[6], (27, C, C), (27 * C) ** -0.5, 0.125),
        "cotangent": normal_values(keys[7], (C, RAD, CELLS), 1.0, 6.0, ((1, 32), (2, 16))),
    }


def pad_grid(field):
    shaped = field.reshape(C, RAD, AZI, INC)
    padded = jnp.pad(shaped, ((0, 0), (1, 1), (0, 0), (1, 1)))
    return jnp.concatenate([padded[:, :, -1:], padded, padded[:, :, :1]], axis=2)

def reference(feats, counts, occupancy, window_ids, w_qkv, w_out, conv_weight, cotangent):
    scale = jnp.log(2.0 + counts.astype(jnp.float32))
    scaled = feats.astype(jnp.float32) * scale[None]
    normed = (scaled * lax.rsqrt(lax.optimization_barrier(jnp.mean(scaled * scaled, axis=0, keepdims=True)) + 1e-05)).astype(jnp.bfloat16)
    qkv = jnp.dot(w_qkv, normed.reshape(C, -1), preferred_element_type=jnp.float32).astype(jnp.bfloat16)
    qkv = qkv.reshape(3, HEADS, HEAD_DIM, RAD, CELLS)
    ids = window_ids.T
    occ_cells = jnp.repeat(occupancy, 128, axis=1)
    tags = jnp.where(occ_cells == 1, ids, -1)
    rows = jnp.arange(RAD, dtype=jnp.int32)
    allowed = (tags[None, :, :] == ids[:, None, :]) | (rows[:, None, None] == rows[None, :, None])

    def one_head(items):
        query, key, value = items
        score = jnp.einsum('drc,dkc->rkc', query.astype(jnp.float32), key.astype(jnp.float32)) * 0.25
        score = jnp.where(allowed, score, -jnp.inf)
        top = lax.optimization_barrier(jnp.max(score, axis=1, keepdims=True))
        weight = jnp.exp(score - top)
        total = lax.optimization_barrier(jnp.sum(weight, axis=1))
        summed = jnp.einsum('rkc,dkc->drc', weight, value.astype(jnp.float32))
        return (summed / total[None]).astype(jnp.bfloat16)
    attn = lax.map(one_head, (qkv[0], qkv[1], qkv[2])).reshape(C, -1)
    mid = (scaled.reshape(C, -1) + jnp.dot(w_out, attn, preferred_element_type=jnp.float32)).astype(jnp.bfloat16)
    mid_pad = pad_grid(mid)
    cot_pad = pad_grid(cotangent)
    cot_flat = cotangent.reshape(C, -1)
    out = jnp.zeros((C, RAD * CELLS), jnp.float32)
    back = jnp.zeros((C, RAD * CELLS), jnp.float32)
    grads = []
    for tap in range(27):
        dr, da, di = (tap // 9, tap // 3 % 3, tap % 3)
        patch = mid_pad[:, dr:dr + RAD, da:da + AZI, di:di + INC].reshape(C, -1)
        out = out + jnp.dot(conv_weight[tap], patch, preferred_element_type=jnp.float32)
        grads.append(lax.dot_general(cot_flat, patch, (((1,), (1,)), ((), ())), preferred_element_type=jnp.float32))
        cpatch = cot_pad[:, 2 - dr:2 - dr + RAD, 2 - da:2 - da + AZI, 2 - di:2 - di + INC].reshape(C, -1)
        back = back + jnp.dot(conv_weight[tap].T, cpatch, preferred_element_type=jnp.float32)
    section_out = out.astype(jnp.bfloat16).reshape(C, RAD, CELLS)
    grad_mid = back.astype(jnp.bfloat16).reshape(C, RAD, CELLS)
    return (section_out, jnp.stack(grads), grad_mid)
```

```python
import jax
import jax.numpy as jnp
from jax import lax
from jax.sharding import Mesh
from jax.sharding import PartitionSpec as P

HEAD_DIM = 16
INC = 32
BAND = ("zh", "y", "x")
SECTOR = ("zl", "c")
PLANE = ("y", "x", "c")
RING = ("zh", "zl")


def all_sum(terms):
    plane, ring = lax.axis_size(PLANE), lax.axis_size(RING)
    shape, size = terms.shape, terms.size
    row = -(-size // (plane * 16 * 128)) * 16
    flat = jnp.pad(terms.reshape(-1).astype(jnp.bfloat16), (0, plane * row * 128 - size))
    got = lax.all_to_all(flat.reshape(plane, row, 128), PLANE, 0, 0, tiled=True)
    mine = jnp.sum(got.astype(jnp.float32), 0).astype(jnp.bfloat16)
    got = lax.all_to_all(jnp.broadcast_to(mine[None], (ring,) + mine.shape), RING, 0, 0, tiled=True)
    mine = jnp.sum(got.astype(jnp.float32), 0).astype(jnp.bfloat16)
    got = lax.all_to_all(
        jnp.broadcast_to(mine[None], (plane,) + mine.shape), PLANE, 0, 0, tiled=True
    )
    return got.reshape(-1)[:size].reshape(shape).astype(jnp.float32)


def extended(cells, sides, width, closed):
    for axis, dim in sides:
        count = lax.axis_size(axis)
        ends = count if closed else count - 1
        head = lax.slice_in_dim(cells, 0, width, axis=dim)
        tail = lax.slice_in_dim(cells, cells.shape[dim] - width, cells.shape[dim], axis=dim)
        cells = jnp.concatenate(
            [
                lax.ppermute(tail, axis, [(i, (i + 1) % count) for i in range(ends)]),
                cells,
                lax.ppermute(head, axis, [((i + 1) % count, i) for i in range(ends)]),
            ],
            axis=dim,
        )
    return cells


def ray_attention(query, key, value, allowed):

    def one_head(items):
        head_query, head_key, head_value = items
        score = (
            jnp.einsum("crd,ckd->crk", head_query, head_key, preferred_element_type=jnp.float32)
            * 0.25
        )
        score = jnp.where(allowed, score, -jnp.inf)
        top = jnp.max(score, axis=2, keepdims=True)
        weight = jnp.exp(score - top)
        total = jnp.sum(weight, axis=2)
        summed = jnp.einsum("crk,ckd->crd", weight, head_value.astype(jnp.float32))
        return (summed / total[..., None]).astype(jnp.bfloat16)

    return lax.map(one_head, (query, key, value))


def shards(feats, counts, occupancy, window_ids, w_qkv, w_out, conv_weight, cotangent):
    chans, rows, cells = feats.shape
    heads = chans // HEAD_DIM
    scale = jnp.log(2.0 + counts.astype(jnp.float32))
    scaled = feats.astype(jnp.float32) * scale[None]
    normed = (scaled * lax.rsqrt(jnp.mean(scaled * scaled, axis=0, keepdims=True) + 1e-05)).astype(
        jnp.bfloat16
    )
    ids = window_ids.T
    occ_cells = jnp.repeat(occupancy, 128, axis=1)
    tags = jnp.where(occ_cells == 1, ids, -1)
    rays = lax.all_to_all(normed, BAND, split_axis=2, concat_axis=1, tiled=True)
    meta = lax.all_to_all(jnp.stack([ids, tags]), BAND, split_axis=2, concat_axis=1, tiled=True)
    full_rows, narrow = (rays.shape[1], rays.shape[2])
    qkv = jnp.dot(w_qkv, rays.reshape(chans, -1), preferred_element_type=jnp.float32).astype(
        jnp.bfloat16
    )
    qkv = qkv.reshape(3, heads, HEAD_DIM, full_rows, narrow).transpose(0, 1, 4, 3, 2)
    ray_ids = meta[0].T
    ray_tags = meta[1].T
    positions = jnp.arange(full_rows, dtype=jnp.int32)
    allowed = (ray_tags[:, None, :] == ray_ids[:, :, None]) | (
        positions[:, None] == positions[None, :]
    )[None]
    ray_out = ray_attention(qkv[0], qkv[1], qkv[2], allowed)
    ray_out = ray_out.transpose(0, 3, 2, 1).reshape(chans, full_rows, narrow)
    attn = lax.all_to_all(ray_out, BAND, split_axis=1, concat_axis=2, tiled=True).reshape(
        chans, -1
    )
    mid = (
        scaled.reshape(chans, -1) + jnp.dot(w_out, attn, preferred_element_type=jnp.float32)
    ).astype(jnp.bfloat16)
    azimuths = cells // INC
    both = jnp.stack(
        [mid.reshape(chans, rows, azimuths, INC), cotangent.reshape(chans, rows, azimuths, INC)]
    )
    both = extended(both, ((SECTOR, 3),), 1, True)
    both = extended(both, ((BAND, 2),), 1, False)
    both = jnp.pad(both, ((0, 0), (0, 0), (0, 0), (0, 0), (1, 1)))
    mid_pad = both[0]
    cot_pad = both[1]
    cot_flat = cotangent.reshape(chans, -1)
    out = jnp.zeros((chans, rows * cells), jnp.float32)
    back = jnp.zeros((chans, rows * cells), jnp.float32)
    grads = []
    for tap in range(27):
        dr, da, di = (tap // 9, tap // 3 % 3, tap % 3)
        patch = mid_pad[:, dr : dr + rows, da : da + azimuths, di : di + INC].reshape(chans, -1)
        out = out + jnp.dot(conv_weight[tap], patch, preferred_element_type=jnp.float32)
        grads.append(
            lax.dot_general(
                cot_flat, patch, (((1,), (1,)), ((), ())), preferred_element_type=jnp.float32
            )
        )
        cpatch = cot_pad[
            :, 2 - dr : 2 - dr + rows, 2 - da : 2 - da + azimuths, 2 - di : 2 - di + INC
        ].reshape(chans, -1)
        back = back + jnp.dot(conv_weight[tap].T, cpatch, preferred_element_type=jnp.float32)
    grad_weight = all_sum(jnp.stack(grads))
    section_out = out.astype(jnp.bfloat16).reshape(chans, rows, cells)
    grad_mid = back.astype(jnp.bfloat16).reshape(chans, rows, cells)
    return (section_out, grad_weight, grad_mid)


def solution(mesh):
    mesh = Mesh(mesh.devices.reshape(2, 4, 4, 8, 2), BAND + SECTOR)
    in_specs = (
        P(None, BAND, SECTOR),
        P(BAND, SECTOR),
        P(BAND, SECTOR),
        P(SECTOR, BAND),
        P(),
        P(),
        P(),
        P(None, BAND, SECTOR),
    )
    out_specs = (P(None, BAND, SECTOR), P(), P(None, BAND, SECTOR))
    return jax.shard_map(shards, mesh=mesh, in_specs=in_specs, out_specs=out_specs, check_vma=False)
```

```python
import jax
import jax.numpy as jnp
from jax import lax
from jax.experimental import pallas as pl
from jax.experimental.pallas import tpu as pltpu
from jax.sharding import Mesh
from jax.sharding import PartitionSpec as P

BF16 = jnp.bfloat16
F32 = jnp.float32
CHANS = 96
HEADS = 6
HEAD_DIM = 16
INC = 32
LANES = 128
TAPS = 27
BAND = ("zh", "y", "x")
SECTOR = ("zl", "c")
FACE = ("y", "x")
PLANE = ("y", "x", "c")
RING = ("zh", "zl")


def whole(kernel, outs, *args):
    return pl.pallas_call(
        kernel,
        out_shape=outs,
        compiler_params=pltpu.CompilerParams(vmem_limit_bytes=32 * 1024 * 1024),
    )(*args)


def dot(a, b):
    return jnp.dot(a, b, preferred_element_type=F32)


def iota(shape, dim):
    return lax.broadcasted_iota(jnp.int32, shape, dim)


def pack_kernel(feats, counts, ids, occupancy, out):
    lane = iota((LANES, LANES), 1)
    rows = []
    for row in range(2):
        cells = jnp.concatenate(
            [feats[row].astype(F32), jnp.zeros((LANES - CHANS, LANES), F32)], axis=0
        ).T
        count = jnp.broadcast_to(counts[row : row + 1, :].astype(F32), (LANES, LANES)).T
        number = ids[:, row : row + 1]
        tag = jnp.where(occupancy[row : row + 1, :] == 1, number, -1).astype(F32)
        cells = jnp.where(lane == CHANS, count, cells)
        cells = jnp.where(lane == CHANS + 1, number.astype(F32), cells)
        cells = jnp.where(lane == CHANS + 2, tag, cells)
        rows.append(cells.reshape(16, 8, LANES))
    out[...] = jnp.concatenate(rows, axis=1).astype(BF16)


def ray_kernel(own, other, w_qkv, w_out, out):
    n = 256

    def prepared(ref):
        cells = ref[...].astype(F32).reshape(n, LANES)
        turned = cells.T
        scaled = turned[:CHANS] * jnp.log(2.0 + turned[CHANS : CHANS + 1])
        square = jnp.sum(scaled * scaled, axis=0, keepdims=True) * (1.0 / CHANS)
        return cells, turned, scaled, (scaled * lax.rsqrt(square + 1e-05)).astype(BF16)

    cells_a, turned_a, scaled, normed_a = prepared(own)
    cells_b, _, _, normed_b = prepared(other)
    qkv_a = dot(w_qkv[...], normed_a)
    kv_b = dot(w_qkv[CHANS:, :], normed_b)
    query = qkv_a[:CHANS].astype(BF16) * 0.25
    key = jnp.concatenate([qkv_a[CHANS : 2 * CHANS].T, kv_b[:CHANS].T], axis=0).astype(BF16)
    value = jnp.concatenate([qkv_a[2 * CHANS :], kv_b[CHANS:]], axis=1).astype(BF16)

    number = turned_a[CHANS + 1 : CHANS + 2].astype(jnp.int32)
    wanted = (iota((1, n), 1) % 8) * 4 + number
    wanted = (iota((32, n), 0) == wanted).astype(F32).astype(BF16)
    tag = jnp.concatenate(
        [cells_a[:, CHANS + 2 : CHANS + 3], cells_b[:, CHANS + 2 : CHANS + 3]], axis=0
    ).astype(jnp.int32)
    given = jnp.where(tag < 0, -1, (iota((2 * n, 1), 0) % 8) * 4 + tag)
    given = (iota((2 * n, 32), 1) == given).astype(F32).astype(BF16)
    allowed = (dot(given, wanted) > 0.5) | (iota((2 * n, n), 0) == iota((2 * n, n), 1))
    bias = jnp.where(allowed, 0.0, -1e30)

    channel = iota((CHANS, n), 0) // HEAD_DIM
    heads = []
    for head in range(HEADS):
        mine = jnp.where(channel == head, query.astype(F32), 0.0).astype(BF16)
        score = dot(key, mine) + bias
        weight = jnp.exp(score - jnp.max(score, axis=0, keepdims=True))
        total = jnp.sum(weight, axis=0, keepdims=True)
        summed = dot(value[head * HEAD_DIM : (head + 1) * HEAD_DIM], weight.astype(BF16))
        heads.append((summed / total).astype(BF16))
    attn = jnp.concatenate(heads, axis=0)
    mid = scaled + dot(w_out[...], attn)
    mid = jnp.concatenate([mid, jnp.zeros((LANES - CHANS, n), F32)], axis=0).T
    out[...] = mid.astype(BF16).reshape(16, 16, LANES)


def shifted_kernel(cot, turned_weight, patches, back):
    rows = cot[...].reshape(4 * CHANS, 6 * INC)
    source, target = iota((6 * INC, LANES), 0), iota((6 * INC, LANES), 1)
    for da in range(3):
        for di in range(3):
            at = target % INC + 1 - di
            move = (source == target + (2 - da) * INC + 1 - di) & (at >= 0) & (at < INC)
            moved = dot(rows, move.astype(F32).astype(BF16)).astype(BF16)
            for dr in range(3):
                tap = dr * 9 + da * 3 + di
                for row in range(2):
                    at_row = (2 - dr + row) * CHANS
                    patches[pl.ds(tap * CHANS, CHANS), pl.ds(row * LANES, LANES)] = moved[
                        at_row : at_row + CHANS
                    ]
    total = dot(turned_weight[...], patches[...]).astype(BF16)
    back[0] = total[:, :LANES]
    back[1] = total[:, LANES:]


def by_rows(cells):
    cells = cells.astype(F32)
    return [cells[:, r * 8 : r * 8 + 8, :].reshape(-1, LANES) for r in range(cells.shape[1] // 8)]


def tap_kernel(patches, mid, out):
    cells = jnp.concatenate(by_rows(mid[...]), axis=0).astype(BF16)
    lane = iota((CHANS, LANES), 1)
    for group in range(7):
        terms = [
            dot(patches[pl.ds(tap * CHANS, CHANS), :], cells)
            for tap in range(group * 4, min(group * 4 + 4, TAPS))
        ]
        for j in range(3):
            tile = terms[j]
            if len(terms) == 4:
                tile = jnp.where(lane < CHANS, tile, pltpu.roll(terms[3], 96 - 32 * j, 1))
            out[pl.ds((group * 3 + j) * CHANS, CHANS), :] = tile.astype(BF16)
    out[pl.ds(21 * CHANS, 32), :] = jnp.zeros((32, LANES), BF16)


def sum_kernel(terms, out):
    total = jnp.sum(terms[...].astype(F32), axis=0, keepdims=True)
    out[...] = jnp.broadcast_to(total, out.shape).astype(BF16)


def unpack_kernel(tiles, out):
    lane = iota((CHANS, LANES), 1)
    for group in range(7):
        parts = [
            tiles[pl.ds((group * 3 + j) * CHANS, CHANS), :].astype(F32) for j in range(3)
        ]
        for j in range(3):
            out[group * 4 + j] = parts[j][:, :CHANS]
        if group * 4 + 3 < TAPS:
            turned = [pltpu.roll(parts[j], 32 + 32 * j, 1) for j in range(3)]
            last = jnp.where(lane < 32, turned[0], jnp.where(lane < 64, turned[1], turned[2]))
            out[group * 4 + 3] = last[:, :CHANS]


def conv_kernel(middle, before, after, weight, out):
    rows = by_rows(before[...]) + by_rows(middle[...]) + by_rows(after[...])
    inc = iota((6 * INC, LANES), 0) % INC
    moved = []
    for row in rows:
        moved.append(
            [
                jnp.where(inc > 0, pltpu.roll(row, 1, 0), 0.0).astype(BF16),
                row.astype(BF16),
                jnp.where(inc < INC - 1, pltpu.roll(row, 6 * INC - 1, 0), 0.0).astype(BF16),
            ]
        )
    for row in range(2):
        total = jnp.zeros((LANES, CHANS), F32)
        for tap in range(TAPS):
            dr, da, di = tap // 9, tap // 3 % 3, tap % 3
            patch = moved[row + dr][di][da * INC : da * INC + LANES, :CHANS]
            total = total + lax.dot_general(
                patch, weight[tap], (((1,), (1,)), ((), ())), preferred_element_type=F32
            )
        out[row] = total.T.astype(BF16)


def exchange(cells, axis):
    return lax.all_to_all(cells, axis, 0, 0, tiled=True)


def ring(count, closed):
    return [(i, (i + 1) % count) for i in range(count if closed else count - 1)]


def back_ring(count, closed):
    return [(j, i) for i, j in ring(count, closed)]


def shards(feats, counts, occupancy, window_ids, w_qkv, w_out, conv_weight, cotangent):
    struct = jax.ShapeDtypeStruct
    cells = struct((16, 16, LANES), BF16)
    mine = whole(pack_kernel, cells, feats.transpose(1, 0, 2), counts, window_ids, occupancy)
    partner = lax.ppermute(mine, "zh", [(0, 1), (1, 0)])
    own = exchange(mine, FACE)
    other = exchange(partner, FACE)

    bands, sectors = lax.axis_size(BAND), lax.axis_size(SECTOR)
    cot = cotangent.transpose(1, 0, 2)
    cot = jnp.concatenate(
        [
            lax.ppermute(cot[:, :, -INC:], SECTOR, ring(sectors, True)),
            cot,
            lax.ppermute(cot[:, :, :INC], SECTOR, back_ring(sectors, True)),
        ],
        axis=2,
    )
    cot = jnp.concatenate(
        [
            lax.ppermute(cot[1:], BAND, ring(bands, False)),
            cot,
            lax.ppermute(cot[:1], BAND, back_ring(bands, False)),
        ],
        axis=0,
    )
    turned_weight = conv_weight.reshape(TAPS * CHANS, CHANS).T
    patches, back = whole(
        shifted_kernel,
        (struct((TAPS * CHANS, 2 * LANES), BF16), struct((2, CHANS, LANES), BF16)),
        cot,
        turned_weight,
    )

    mid = exchange(whole(ray_kernel, cells, own, other, w_qkv, w_out), FACE)

    plane, along = lax.axis_size(PLANE), lax.axis_size(RING)
    terms = whole(tap_kernel, struct((2048, LANES), BF16), patches, mid)
    terms = exchange(terms.reshape(plane, -1, LANES), PLANE)
    part = terms.shape[1:]
    terms = exchange(whole(sum_kernel, struct((along,) + part, BF16), terms), RING)
    terms = exchange(whole(sum_kernel, struct((plane,) + part, BF16), terms), PLANE)
    grad_weight = whole(
        unpack_kernel, struct((TAPS, CHANS, CHANS), F32), terms.reshape(2048, LANES)
    )

    wide = jnp.concatenate(
        [
            lax.ppermute(mid[-4:], SECTOR, ring(sectors, True)),
            mid,
            lax.ppermute(mid[:4], SECTOR, back_ring(sectors, True)),
        ],
        axis=0,
    )
    before = lax.ppermute(wide[:, 8:], BAND, ring(bands, False))
    after = lax.ppermute(wide[:, :8], BAND, back_ring(bands, False))
    out = whole(conv_kernel, struct((2, CHANS, LANES), BF16), wide, before, after, conv_weight)
    return (out.transpose(1, 0, 2), grad_weight, back.transpose(1, 0, 2))


def solution(mesh):
    mesh = Mesh(mesh.devices.reshape(2, 4, 4, 8, 2), BAND + SECTOR)
    in_specs = (
        P(None, BAND, SECTOR),
        P(BAND, SECTOR),
        P(BAND, SECTOR),
        P(SECTOR, BAND),
        P(),
        P(),
        P(),
        P(None, BAND, SECTOR),
    )
    out_specs = (P(None, BAND, SECTOR), P(), P(None, BAND, SECTOR))
    return jax.shard_map(shards, mesh=mesh, in_specs=in_specs, out_specs=out_specs, check_vma=False)
```

```python
import jax
import jax.numpy as jnp
from jax import lax
from jax.experimental import pallas as pl
from jax.experimental.pallas import tpu as pltpu
from jax.sharding import Mesh
from jax.sharding import PartitionSpec as P

BF16 = jnp.bfloat16
F32 = jnp.float32
CHANS = 96
HEADS = 6
HEAD_DIM = 16
INC = 32
LANES = 128
TAPS = 27
BAND = ("zh", "y", "x")
SECTOR = ("zl", "c")
FACE = ("y", "x")
PLANE = ("y", "x", "c")
RING = ("zh", "zl")


def whole(kernel, outs, *args):
    return pl.pallas_call(
        kernel,
        out_shape=outs,
        compiler_params=pltpu.CompilerParams(vmem_limit_bytes=32 * 1024 * 1024),
    )(*args)


def dot(a, b):
    return jnp.dot(a, b, preferred_element_type=F32)


def iota(shape, dim):
    return lax.broadcasted_iota(jnp.int32, shape, dim)


def pack_kernel(feats_hbm, counts_hbm, ids_hbm, occupancy_hbm, out, feats, counts, ids, occupancy, sems):
    copies = [
        pltpu.make_async_copy(source, target, sems.at[i])
        for i, (source, target) in enumerate(
            [
                (feats_hbm, feats),
                (counts_hbm, counts),
                (ids_hbm, ids),
                (occupancy_hbm, occupancy),
            ]
        )
    ]
    for copy in copies:
        copy.start()
    for copy in copies:
        copy.wait()
    lane = iota((LANES, LANES), 1)
    both = feats[...].astype(F32)
    rows = []
    for row in range(2):
        number = ids[row : row + 1, :]
        tag = jnp.where(occupancy[:, row : row + 1] == 1, number, -1)
        more = [v.astype(F32) for v in (counts[row : row + 1, :], number, tag)]
        more.append(jnp.zeros((LANES - CHANS - 3, LANES), F32))
        cells = jnp.concatenate([both[:, row, :]] + more, axis=0)
        rows.append(cells.T.reshape(16, 8, LANES))
    out[...] = jnp.concatenate(rows, axis=1).astype(BF16)


def ray_kernel(place_of, loads, w_qkv_hbm, w_out_hbm, turned_weight, out, w_qkv, w_out, patches, sems):
    n, wide = 256, 384
    fetches = [
        pltpu.make_async_copy(w_qkv_hbm, w_qkv, sems.at[0]),
        pltpu.make_async_copy(w_out_hbm, w_out, sems.at[1]),
    ]
    for fetch in fetches:
        fetch.start()
    every = loads[...].astype(F32)
    own = every[:, :16].reshape(n, LANES)
    other = every[:, 16:32].reshape(n, LANES)
    low = place_of[0, 0] == 0
    edge = jnp.where(low, other[:8], other[n - 8 :])
    asked = jnp.concatenate([own, edge, jnp.zeros((wide - n - 8, LANES), F32)], axis=0)

    def prepared(cells):
        turned = cells.T
        scaled = turned[:CHANS] * jnp.log(2.0 + turned[CHANS : CHANS + 1])
        square = jnp.sum(scaled * scaled, axis=0, keepdims=True) * (1.0 / CHANS)
        return turned, scaled, (scaled * lax.rsqrt(square + 1e-05)).astype(BF16)

    turned, scaled, normed_a = prepared(asked)
    _, _, normed_b = prepared(other)
    for fetch in fetches:
        fetch.wait()
    query = dot(w_qkv[:CHANS, :], normed_a).astype(BF16).astype(F32) * 0.25
    kv = dot(w_qkv[CHANS:, :], jnp.concatenate([normed_a[:, :n], normed_b], axis=1))
    key = kv[:CHANS].T.astype(BF16)
    value = kv[CHANS:].astype(BF16)

    number = turned[CHANS + 1 : CHANS + 2].astype(jnp.int32)
    wanted = (iota((1, wide), 1) % 8) * 4 + number
    wanted = (iota((32, wide), 0) == wanted).astype(F32).astype(BF16)
    tag = jnp.concatenate(
        [own[:, CHANS + 2 : CHANS + 3], other[:, CHANS + 2 : CHANS + 3]], axis=0
    ).astype(jnp.int32)
    given = jnp.where(tag < 0, -1, (iota((2 * n, 1), 0) % 8) * 4 + tag)
    given = (iota((2 * n, 32), 1) == given).astype(F32).astype(BF16)
    place = iota((1, wide), 1)
    place = jnp.where((place < n) | low, place, place + n - 8)
    allowed = (dot(given, wanted) > 0.5) | (iota((2 * n, wide), 0) == place)
    bias = jnp.where(allowed, 0.0, -1e30)

    cell = iota((16, 8, LANES), 1)
    for da in range(3):
        shifted = [[], [], []]
        for row in range(2):
            at, edge_at = 32 + da * 16 + row * 8, 80 + da * 4 + row * 2
            block = every[:, at : at + 8]
            flat = block.reshape(LANES, LANES)
            upper = pltpu.roll(flat, LANES - 1, 0).reshape(16, 8, LANES)
            lower = pltpu.roll(flat, 1, 0).reshape(16, 8, LANES)
            shifted[0].append(jnp.where(cell < 7, upper, every[:, edge_at + 1 : edge_at + 2]))
            shifted[1].append(block)
            shifted[2].append(jnp.where(cell > 0, lower, every[:, edge_at : edge_at + 1]))
        for di in range(3):
            cells = jnp.concatenate(shifted[di], axis=1).reshape(n, LANES)
            patches[pl.ds((da * 3 + di) * CHANS, CHANS), :] = cells.T[:CHANS].astype(BF16)

    channel = iota((CHANS, wide), 0) // HEAD_DIM
    heads = []
    for head in range(HEADS):
        mine = jnp.where(channel == head, query, 0.0).astype(BF16)
        score = dot(key, mine) + bias
        weight = jnp.exp(score - jnp.max(score, axis=0, keepdims=True))
        total = jnp.sum(weight, axis=0, keepdims=True)
        summed = dot(value[head * HEAD_DIM : (head + 1) * HEAD_DIM], weight.astype(BF16))
        heads.append((summed / total).astype(BF16))
    attn = jnp.concatenate(heads, axis=0)
    mid = scaled + dot(w_out[...], attn)
    mid = jnp.concatenate([mid, jnp.zeros((LANES - CHANS, wide), F32)], axis=0).T
    edge, none = mid[n : n + 8], jnp.zeros((8, LANES), F32)
    mid = jnp.concatenate(
        [jnp.where(low, none, edge), mid[:n], jnp.where(low, edge, none)], axis=0
    )
    pairs = mid.reshape(17, 16, LANES)
    pairs = jnp.concatenate([pairs[:16], pairs[1:]], axis=1).astype(BF16)

    near = [mid[8 * dr : 8 * dr + n].astype(BF16) for dr in range(3)]
    lane = iota((CHANS, LANES), 1)
    for group in range(7):
        parts = [
            dot(patches[pl.ds(tap % 9 * CHANS, CHANS), :], near[tap // 9])
            for tap in range(group * 4, min(group * 4 + 4, TAPS))
        ]
        for j in range(3):
            tile = parts[j]
            if len(parts) == 4:
                tile = jnp.where(lane < CHANS, tile, pltpu.roll(parts[3], 96 - 32 * j, 1))
            tile = tile.astype(BF16)
            for q in range(3):
                at = (group * 3 + j) * CHANS + 32 * q
                out[at // 64, pl.ds(at % 64, 32), :] = tile[32 * q : 32 * q + 32]
    out[31, pl.ds(32, 32), :] = jnp.zeros((32, LANES), BF16)

    lane = iota((CHANS, n), 1)
    up, level, down = (dot(turned_weight[dr], patches[...]) for dr in range(3))
    back = level + jnp.where(lane < n - 8, pltpu.roll(up, n - 8, 1), 0.0)
    back = back + jnp.where(lane >= 8, pltpu.roll(down, 8, 1), 0.0)
    back = jnp.concatenate([back, jnp.zeros((LANES - CHANS, n), F32)], axis=0).T
    back = back.astype(BF16).reshape(16, 16, LANES)
    for face in range(16):
        for core in range(2):
            out[2 * face + core, pl.ds(64, 32), :] = pairs[face]
            out[2 * face + core, pl.ds(96, 16), :] = back[face]


def moves():
    source, target = iota((6 * INC, LANES), 0), iota((6 * INC, LANES), 1)
    for da in range(3):
        for di in range(3):
            at = target % INC + 1 - di
            move = (source == target + (2 - da) * INC + 1 - di) & (at >= 0) & (at < INC)
            yield da, di, move.astype(F32).astype(BF16)


def load_kernel(mine, partner, left, middle, right, out):
    inc = iota((6 * INC, LANES), 0) % INC
    rows = []
    for row in range(2):
        parts = []
        for piece in (left, middle, right):
            cells = piece[row].astype(F32)
            more = jnp.zeros((LANES - CHANS, cells.shape[1]), F32)
            parts.append(jnp.concatenate([cells, more], axis=0).T)
        cells = jnp.concatenate(parts, axis=0)
        lower = jnp.where(inc > 0, pltpu.roll(cells, 1, 0), 0.0)
        upper = jnp.where(inc < INC - 1, pltpu.roll(cells, 6 * INC - 1, 0), 0.0)
        rows.append((cells, lower, upper))
    blocks, edges = [], []
    for da in range(3):
        at = (2 - da) * INC
        for row in range(2):
            cells, lower, upper = (v[at : at + LANES].reshape(16, 8, LANES) for v in rows[row])
            blocks.append(cells)
            edges += [lower[:, :1], upper[:, 7:]]
    edges.append(jnp.zeros((16, 4, LANES), F32))
    out[:, pl.ds(0, 16), :] = mine[...]
    out[:, pl.ds(16, 16), :] = partner[...]
    out[:, pl.ds(32, 48), :] = jnp.concatenate(blocks, axis=1).astype(BF16)
    out[:, pl.ds(80, 16), :] = jnp.concatenate(edges, axis=1).astype(BF16)


def by_rows(cells):
    cells = cells.astype(F32)
    return [cells[:, r * 8 : r * 8 + 8, :].reshape(-1, LANES) for r in range(cells.shape[1] // 8)]


def sum_kernel(terms, out):
    total = jnp.sum(terms[:, pl.ds(0, 64), :].astype(F32), axis=0, keepdims=True)
    out[...] = jnp.broadcast_to(total, out.shape).astype(BF16)


def unpack_kernel(tiles, out):
    lane = iota((CHANS, LANES), 1)
    for group in range(7):
        parts = [
            tiles[pl.ds((group * 3 + j) * CHANS, CHANS), :].astype(F32) for j in range(3)
        ]
        for j in range(3):
            out[group * 4 + j] = parts[j][:, :CHANS]
        if group * 4 + 3 < TAPS:
            turned = [pltpu.roll(parts[j], 32 + 32 * j, 1) for j in range(3)]
            last = jnp.where(lane < 32, turned[0], jnp.where(lane < 64, turned[1], turned[2]))
            out[group * 4 + 3] = last[:, :CHANS]


def conv_kernel(place_of, blocks, halo, far, weight, turned_weight, out, back, patches):
    low, first = place_of[0, 0] == 0, place_of[0, 1] == 0
    got = blocks[:, pl.ds(64, 48), :].astype(F32).reshape(16, 2, 48, LANES)
    mine = jnp.where(first, got[:, 0], got[:, 1])
    beside = jnp.where(first, got[:4, 1, :32], got[12:, 0, :32])
    edge = halo[...].astype(F32)
    left, right = jnp.where(first, edge, beside), jnp.where(first, beside, edge)

    for da, di, move in moves():
        patches[pl.ds((da * 3 + di) * CHANS, CHANS), :] = dot(far[0], move).astype(BF16)
    more = [dot(turned_weight[dr], patches[...]) for dr in (2, 0)]
    more = [jnp.where(low, 0.0, more[0]), jnp.where(low, more[1], 0.0)]
    for row, cells in enumerate(by_rows(mine[:, 32:])):
        back[row] = (cells.T[:CHANS] + more[row]).astype(BF16)

    rows = by_rows(jnp.concatenate([left, mine[:, :32], right], axis=0))
    inc = iota((6 * INC, LANES), 0) % INC
    moved = []
    for row in rows:
        moved.append(
            [
                jnp.where(inc > 0, pltpu.roll(row, 1, 0), 0.0).astype(BF16),
                row.astype(BF16),
                jnp.where(inc < INC - 1, pltpu.roll(row, 6 * INC - 1, 0), 0.0).astype(BF16),
            ]
        )
    for row in range(2):
        total = jnp.zeros((LANES, CHANS), F32)
        for tap in range(TAPS):
            dr, da, di = tap // 9, tap // 3 % 3, tap % 3
            patch = moved[row + dr][di][da * INC : da * INC + LANES, :CHANS]
            total = total + lax.dot_general(
                patch, weight[tap], (((1,), (1,)), ((), ())), preferred_element_type=F32
            )
        out[row] = total.T.astype(BF16)


def exchange(cells, axis):
    return lax.all_to_all(cells, axis, 0, 0, tiled=True)


def ring(count, closed):
    return [(i, (i + 1) % count) for i in range(count if closed else count - 1)]


def back_ring(count, closed):
    return [(j, i) for i, j in ring(count, closed)]


def shards(feats, counts, occupancy, window_ids, w_qkv, w_out, conv_weight, cotangent):
    struct = jax.ShapeDtypeStruct
    sectors = lax.axis_size(SECTOR)
    mine = pl.pallas_call(
        pack_kernel,
        out_shape=struct((16, 16, LANES), BF16),
        in_specs=[pl.BlockSpec(memory_space=pl.ANY)] * 4,
        scratch_shapes=[
            pltpu.VMEM((CHANS, 2, LANES), BF16),
            pltpu.VMEM((2, LANES), jnp.int32),
            pltpu.VMEM((2, LANES), jnp.int32),
            pltpu.VMEM((1, 2), jnp.int32),
            pltpu.SemaphoreType.DMA((4,)),
        ],
    )(feats, counts, window_ids.T, occupancy.T)
    partner = lax.ppermute(mine, "zh", [(0, 1), (1, 0)])
    cotangent, mine = lax.optimization_barrier((cotangent, mine))
    cot = cotangent.transpose(1, 0, 2)
    left = lax.ppermute(cot[:, :, -INC:], SECTOR, ring(sectors, True))
    right = lax.ppermute(cot[:, :, :INC], SECTOR, back_ring(sectors, True))
    loads = whole(load_kernel, struct((16, 96, LANES), BF16), mine, partner, left, cot, right)
    loads = exchange(loads, FACE)
    turned_weight = conv_weight.reshape(3, 9 * CHANS, CHANS).transpose(0, 2, 1)

    side, core = lax.axis_index("zh"), lax.axis_index("c")
    place_of = jnp.stack([side, core]).astype(jnp.int32).reshape(1, 2)
    smem, vmem = pl.BlockSpec(memory_space=pltpu.SMEM), pl.BlockSpec(memory_space=pltpu.VMEM)
    hbm = pl.BlockSpec(memory_space=pl.ANY)
    params = pltpu.CompilerParams(vmem_limit_bytes=32 * 1024 * 1024)
    plane, along, face = lax.axis_size(PLANE), lax.axis_size(RING), lax.axis_size(FACE)
    blocks = pl.pallas_call(
        ray_kernel,
        out_shape=struct((plane, 112, LANES), BF16),
        in_specs=[smem, vmem, hbm, hbm, vmem],
        scratch_shapes=[
            pltpu.VMEM((3 * CHANS, CHANS), BF16),
            pltpu.VMEM((CHANS, CHANS), BF16),
            pltpu.VMEM((9 * CHANS, 2 * LANES), BF16),
            pltpu.SemaphoreType.DMA((2,)),
        ],
        compiler_params=params,
    )(place_of, loads, w_qkv, w_out, turned_weight)
    blocks = exchange(blocks, PLANE)

    terms = whole(sum_kernel, struct((along, 64, LANES), BF16), blocks)
    terms, blocks, cot, left, right = lax.optimization_barrier((terms, blocks, cot, left, right))
    terms = whole(sum_kernel, struct((plane, 64, LANES), BF16), exchange(terms, RING))

    edge = lax.dynamic_slice(
        blocks.reshape(face, 2, 112, LANES), (12 * core, core, 64, 0), (4, 1, 32, LANES)
    ).reshape(4, 32, LANES)
    odd = [(i, (i + 1) % sectors) for i in range(1, sectors, 2)]
    halo = lax.ppermute(edge, SECTOR, odd + [(j, i) for i, j in odd])
    far = jnp.concatenate([left, cot, right], axis=2)
    far = jnp.where(side == 0, far[1:], far[:1])
    far = lax.ppermute(far, BAND, [(face - 1, face), (face, face - 1)])
    out, back = pl.pallas_call(
        conv_kernel,
        out_shape=(struct((2, CHANS, LANES), BF16),) * 2,
        in_specs=[smem] + [vmem] * 5,
        scratch_shapes=[pltpu.VMEM((9 * CHANS, LANES), BF16)],
        compiler_params=params,
    )(place_of, blocks, halo, far, conv_weight, turned_weight)
    out, back = out.transpose(1, 0, 2), back.transpose(1, 0, 2)

    terms, out, back = lax.optimization_barrier((terms, out, back))
    grad_weight = whole(
        unpack_kernel,
        struct((TAPS, CHANS, CHANS), F32),
        exchange(terms, PLANE).reshape(2048, LANES),
    )
    return (out, grad_weight, back)


def solution(mesh):
    mesh = Mesh(mesh.devices.reshape(2, 4, 4, 8, 2), BAND + SECTOR)
    in_specs = (
        P(None, BAND, SECTOR),
        P(BAND, SECTOR),
        P(BAND, SECTOR),
        P(SECTOR, BAND),
        P(),
        P(),
        P(),
        P(None, BAND, SECTOR),
    )
    out_specs = (P(None, BAND, SECTOR), P(), P(None, BAND, SECTOR))
    return jax.shard_map(shards, mesh=mesh, in_specs=in_specs, out_specs=out_specs, check_vma=False)
```

```python
import jax
import jax.numpy as jnp
from jax import lax
from jax.experimental import pallas as pl
from jax.experimental.pallas import tpu as pltpu
from jax.sharding import Mesh
from jax.sharding import PartitionSpec as P

BF16 = jnp.bfloat16
F32 = jnp.float32
CHANS = 96
HEADS = 6
HEAD_DIM = 16
INC = 32
LANES = 128
TAPS = 27
BAND = ("zh", "y", "x")
SECTOR = ("zl", "c")
FACE = ("y", "x")
PLANE = ("y", "x", "c")
RING = ("zh", "zl")


def whole(kernel, outs, *args):
    return pl.pallas_call(
        kernel,
        out_shape=outs,
        compiler_params=pltpu.CompilerParams(vmem_limit_bytes=32 * 1024 * 1024),
    )(*args)


def dot(a, b):
    return jnp.dot(a, b, preferred_element_type=F32)


def iota(shape, dim):
    return lax.broadcasted_iota(jnp.int32, shape, dim)


def lower_half():
    return lax.axis_index("zh") == 0


def first_core():
    return lax.axis_index("c") == 0


def pack_kernel(
    feats_hbm, counts_hbm, ids_hbm, occupancy_hbm, cot_hbm,
    out, turned, to_core, to_chip, feats, counts, ids, occupancy, cot, sems,
):
    pairs = [
        (feats_hbm, feats),
        (counts_hbm, counts),
        (ids_hbm, ids),
        (occupancy_hbm, occupancy),
        (cot_hbm, cot),
    ]
    copies = [pltpu.make_async_copy(*pair, sems.at[i]) for i, pair in enumerate(pairs)]
    for copy in copies:
        copy.start()
    for copy in copies:
        copy.wait()
    both, each = feats[...].astype(F32), cot[...].astype(F32)
    more = []
    for row in range(2):
        out[pl.ds(row * CHANS, CHANS), :] = both[:, row, :].astype(BF16)
        cells = each[:, row, :].astype(BF16)
        turned[row] = cells
        head, tail = each[:, row, :INC], each[:, row, LANES - INC :]
        to_core[row] = jnp.where(first_core(), tail, head).astype(BF16)
        to_chip[row] = jnp.where(first_core(), head, tail).astype(BF16)
        number = ids[row : row + 1, :]
        tag = jnp.where(occupancy[:, row : row + 1] == 1, number, -1)
        more += [v.astype(F32) for v in (counts[row : row + 1, :], number, tag)]
        more.append(jnp.zeros((5, LANES), F32))
    out[pl.ds(2 * CHANS, 16), :] = jnp.concatenate(more, axis=0).astype(BF16)
    edge = jnp.where(lower_half(), each[:, 1, :], each[:, 0, :])
    out[pl.ds(2 * CHANS + 16, CHANS), :] = edge.astype(BF16)


def ray_kernel(loads, w_qkv_hbm, w_out_hbm, turned_weight, out, w_qkv, w_out, patches, sems):
    n, wide = 256, 384
    fetches = [
        pltpu.make_async_copy(w_qkv_hbm, w_qkv, sems.at[0]),
        pltpu.make_async_copy(w_out_hbm, w_out, sems.at[1]),
    ]
    for fetch in fetches:
        fetch.start()
    every = loads[...].astype(F32)
    own = every[:, :16].reshape(n, LANES)
    other = every[:, 16:32].reshape(n, LANES)
    low = lower_half()
    edge = jnp.where(low, other[:8], other[n - 8 :])
    asked = jnp.concatenate([own, edge, jnp.zeros((wide - n - 8, LANES), F32)], axis=0)

    def prepared(cells):
        turned = cells.T
        scaled = turned[:CHANS] * jnp.log(2.0 + turned[CHANS : CHANS + 1])
        square = jnp.sum(scaled * scaled, axis=0, keepdims=True) * (1.0 / CHANS)
        return turned, scaled, (scaled * lax.rsqrt(square + 1e-05)).astype(BF16)

    turned, scaled, normed_a = prepared(asked)
    _, _, normed_b = prepared(other)
    for fetch in fetches:
        fetch.wait()
    query = dot(w_qkv[:CHANS, :], normed_a).astype(BF16).astype(F32) * 0.25
    kv = dot(w_qkv[CHANS:, :], jnp.concatenate([normed_a[:, :n], normed_b], axis=1))
    key = kv[:CHANS].T.astype(BF16)
    value = kv[CHANS:].astype(BF16)

    number = turned[CHANS + 1 : CHANS + 2].astype(jnp.int32)
    wanted = (iota((1, wide), 1) % 8) * 4 + number
    wanted = (iota((32, wide), 0) == wanted).astype(F32).astype(BF16)
    tag = jnp.concatenate(
        [own[:, CHANS + 2 : CHANS + 3], other[:, CHANS + 2 : CHANS + 3]], axis=0
    ).astype(jnp.int32)
    given = jnp.where(tag < 0, -1, (iota((2 * n, 1), 0) % 8) * 4 + tag)
    given = (iota((2 * n, 32), 1) == given).astype(F32).astype(BF16)
    place = iota((1, wide), 1)
    place = jnp.where((place < n) | low, place, place + n - 8)
    allowed = (dot(given, wanted) > 0.5) | (iota((2 * n, wide), 0) == place)
    bias = jnp.where(allowed, 0.0, -1e30)

    cell = iota((16, 8, LANES), 1)
    for da in range(3):
        shifted = [[], [], []]
        for row in range(2):
            at, edge_at = 32 + da * 16 + row * 8, 80 + da * 4 + row * 2
            block = every[:, at : at + 8]
            flat = block.reshape(LANES, LANES)
            upper = pltpu.roll(flat, LANES - 1, 0).reshape(16, 8, LANES)
            lower = pltpu.roll(flat, 1, 0).reshape(16, 8, LANES)
            shifted[0].append(jnp.where(cell < 7, upper, every[:, edge_at + 1 : edge_at + 2]))
            shifted[1].append(block)
            shifted[2].append(jnp.where(cell > 0, lower, every[:, edge_at : edge_at + 1]))
        for di in range(3):
            cells = jnp.concatenate(shifted[di], axis=1).reshape(n, LANES)
            patches[pl.ds((da * 3 + di) * CHANS, CHANS), :] = cells.T[:CHANS].astype(BF16)

    channel = iota((CHANS, wide), 0) // HEAD_DIM
    heads = []
    for head in range(HEADS):
        mine = jnp.where(channel == head, query, 0.0).astype(BF16)
        score = dot(key, mine) + bias
        weight = jnp.exp(score - jnp.max(score, axis=0, keepdims=True))
        total = jnp.sum(weight, axis=0, keepdims=True)
        summed = dot(value[head * HEAD_DIM : (head + 1) * HEAD_DIM], weight.astype(BF16))
        heads.append((summed / total).astype(BF16))
    attn = jnp.concatenate(heads, axis=0)
    mid = scaled + dot(w_out[...], attn)
    mid = jnp.concatenate([mid, jnp.zeros((LANES - CHANS, wide), F32)], axis=0).T
    edge, none = mid[n : n + 8], jnp.zeros((8, LANES), F32)
    mid = jnp.concatenate(
        [jnp.where(low, none, edge), mid[:n], jnp.where(low, edge, none)], axis=0
    )
    pairs = mid.reshape(17, 16, LANES)
    pairs = jnp.concatenate([pairs[:16], pairs[1:]], axis=1).astype(BF16)

    near = [mid[8 * dr : 8 * dr + n].astype(BF16) for dr in range(3)]
    lane = iota((CHANS, LANES), 1)
    for group in range(7):
        parts = [
            dot(patches[pl.ds(tap % 9 * CHANS, CHANS), :], near[tap // 9])
            for tap in range(group * 4, min(group * 4 + 4, TAPS))
        ]
        for j in range(3):
            tile = parts[j]
            if len(parts) == 4:
                tile = jnp.where(lane < CHANS, tile, pltpu.roll(parts[3], 96 - 32 * j, 1))
            tile = tile.astype(BF16)
            for q in range(3):
                at = (group * 3 + j) * CHANS + 32 * q
                out[at // 64, pl.ds(at % 64, 32), :] = tile[32 * q : 32 * q + 32]
    out[31, pl.ds(32, 32), :] = jnp.zeros((32, LANES), BF16)

    lane = iota((CHANS, n), 1)
    up, level, down = (dot(turned_weight[dr], patches[...]) for dr in range(3))
    back = level + jnp.where(lane < n - 8, pltpu.roll(up, n - 8, 1), 0.0)
    back = back + jnp.where(lane >= 8, pltpu.roll(down, 8, 1), 0.0)
    back = jnp.concatenate([back, jnp.zeros((LANES - CHANS, n), F32)], axis=0).T
    back = back.astype(BF16).reshape(16, 16, LANES)
    for face in range(16):
        for core in range(2):
            out[2 * face + core, pl.ds(64, 32), :] = pairs[face]
            out[2 * face + core, pl.ds(96, 16), :] = back[face]


def moves():
    source, target = iota((6 * INC, LANES), 0), iota((6 * INC, LANES), 1)
    for da in range(3):
        for di in range(3):
            at = target % INC + 1 - di
            move = (source == target + (2 - da) * INC + 1 - di) & (at >= 0) & (at < INC)
            yield da, di, move.astype(F32).astype(BF16)


def load_kernel(mine_hbm, partner_hbm, middle, from_core, from_chip, out, mine, partner, sems):
    copies = [
        pltpu.make_async_copy(mine_hbm, mine, sems.at[0]),
        pltpu.make_async_copy(partner_hbm, partner, sems.at[1]),
    ]
    for copy in copies:
        copy.start()
    inc = iota((6 * INC, LANES), 0) % INC
    rows = []
    for row in range(2):
        parts = []
        core, chip = from_core[row].astype(F32), from_chip[row].astype(F32)
        left, right = jnp.where(first_core(), chip, core), jnp.where(first_core(), core, chip)
        for cells in (left, middle[row].astype(F32), right):
            more = jnp.zeros((LANES - CHANS, cells.shape[1]), F32)
            parts.append(jnp.concatenate([cells, more], axis=0).T)
        cells = jnp.concatenate(parts, axis=0)
        lower = jnp.where(inc > 0, pltpu.roll(cells, 1, 0), 0.0)
        upper = jnp.where(inc < INC - 1, pltpu.roll(cells, 6 * INC - 1, 0), 0.0)
        rows.append((cells, lower, upper))
    blocks, edges = [], []
    for da in range(3):
        at = (2 - da) * INC
        for row in range(2):
            cells, lower, upper = (v[at : at + LANES].reshape(16, 8, LANES) for v in rows[row])
            blocks.append(cells)
            edges += [lower[:, :1], upper[:, 7:]]
    edges.append(jnp.zeros((16, 4, LANES), F32))
    for copy in copies:
        copy.wait()
    for half, packed in enumerate((mine, partner)):
        voxels = []
        for row in range(2):
            parts = [
                packed[pl.ds(row * CHANS, CHANS), :].astype(F32),
                packed[pl.ds(2 * CHANS, 16), :].astype(F32)[row * 8 : row * 8 + 8],
                jnp.zeros((LANES - CHANS - 8, LANES), F32),
            ]
            voxels.append(jnp.concatenate(parts, axis=0).T.reshape(16, 8, LANES))
        out[:, pl.ds(half * 16, 16), :] = jnp.concatenate(voxels, axis=1).astype(BF16)
    out[:, pl.ds(32, 48), :] = jnp.concatenate(blocks, axis=1).astype(BF16)
    out[:, pl.ds(80, 16), :] = jnp.concatenate(edges, axis=1).astype(BF16)


def by_rows(cells):
    cells = cells.astype(F32)
    return [cells[:, r * 8 : r * 8 + 8, :].reshape(-1, LANES) for r in range(cells.shape[1] // 8)]


def sum_kernel(terms, out):
    total = jnp.sum(terms[:, pl.ds(0, 64), :].astype(F32), axis=0, keepdims=True)
    out[...] = jnp.broadcast_to(total, out.shape).astype(BF16)


def unpack_kernel(tiles, out):
    lane = iota((CHANS, LANES), 1)
    for group in range(7):
        parts = [
            tiles[pl.ds((group * 3 + j) * CHANS, CHANS), :].astype(F32) for j in range(3)
        ]
        for j in range(3):
            out[group * 4 + j] = parts[j][:, :CHANS]
        if group * 4 + 3 < TAPS:
            turned = [pltpu.roll(parts[j], 32 + 32 * j, 1) for j in range(3)]
            last = jnp.where(lane < 32, turned[0], jnp.where(lane < 64, turned[1], turned[2]))
            out[group * 4 + 3] = last[:, :CHANS]


def conv_kernel(blocks, halo, far, from_core, weight, turned_weight, out, back, patches):
    low, first = lower_half(), first_core()
    got = blocks[:, pl.ds(64, 48), :].astype(F32).reshape(16, 2, 48, LANES)
    mine = jnp.where(first, got[:, 0], got[:, 1])
    beside = jnp.where(first, got[:4, 1, :32], got[12:, 0, :32])
    edge = halo[pl.ds(0, LANES), :].astype(F32).reshape(4, 32, LANES)
    left, right = jnp.where(first, edge, beside), jnp.where(first, beside, edge)

    core, chip = from_core[...].astype(F32), halo[pl.ds(LANES, CHANS), :].astype(F32)
    before, after = jnp.where(first, chip, core), jnp.where(first, core, chip)
    beyond = [before[:, LANES - INC :], far[...].astype(F32), after[:, :INC]]
    at = lax.axis_index("y") * lax.axis_size("x") + lax.axis_index("x")
    reached = at == jnp.where(low, 15, 0)
    beyond = jnp.where(reached, jnp.concatenate(beyond, axis=1), 0.0).astype(BF16)
    for da, di, move in moves():
        patches[pl.ds((da * 3 + di) * CHANS, CHANS), :] = dot(beyond, move).astype(BF16)
    more = [dot(turned_weight[dr], patches[...]) for dr in (2, 0)]
    more = [jnp.where(low, 0.0, more[0]), jnp.where(low, more[1], 0.0)]
    for row, cells in enumerate(by_rows(mine[:, 32:])):
        back[row] = (cells.T[:CHANS] + more[row]).astype(BF16)

    rows = by_rows(jnp.concatenate([left, mine[:, :32], right], axis=0))
    inc = iota((6 * INC, LANES), 0) % INC
    moved = []
    for row in rows:
        moved.append(
            [
                jnp.where(inc > 0, pltpu.roll(row, 1, 0), 0.0).astype(BF16),
                row.astype(BF16),
                jnp.where(inc < INC - 1, pltpu.roll(row, 6 * INC - 1, 0), 0.0).astype(BF16),
            ]
        )
    for row in range(2):
        total = jnp.zeros((LANES, CHANS), F32)
        for tap in range(TAPS):
            dr, da, di = tap // 9, tap // 3 % 3, tap % 3
            patch = moved[row + dr][di][da * INC : da * INC + LANES, :CHANS]
            total = total + lax.dot_general(
                patch, weight[tap], (((1,), (1,)), ((), ())), preferred_element_type=F32
            )
        out[row] = total.T.astype(BF16)


def exchange(cells, axis):
    return lax.all_to_all(cells, axis, 0, 0, tiled=True)


def shards(feats, counts, occupancy, window_ids, w_qkv, w_out, conv_weight, cotangent):
    struct = jax.ShapeDtypeStruct
    sectors = lax.axis_size(SECTOR)
    core = lax.axis_index("c")
    plane, along, face = lax.axis_size(PLANE), lax.axis_size(RING), lax.axis_size(FACE)
    vmem, hbm = pl.BlockSpec(memory_space=pltpu.VMEM), pl.BlockSpec(memory_space=pl.ANY)
    params = pltpu.CompilerParams(vmem_limit_bytes=32 * 1024 * 1024)
    chips = [(i, (i + 1) % sectors) for i in range(1, sectors, 2)]
    chips += [(j, i) for i, j in chips]
    swap = [(0, 1), (1, 0)]
    packed, edge = (3 * CHANS + 16, LANES), struct((2, CHANS, INC), BF16)
    mine, cot, to_core, to_chip = pl.pallas_call(
        pack_kernel,
        out_shape=(struct(packed, BF16), struct((2, CHANS, LANES), BF16), edge, edge),
        in_specs=[hbm] * 5,
        scratch_shapes=[
            pltpu.VMEM((CHANS, 2, LANES), BF16),
            pltpu.VMEM((2, LANES), jnp.int32),
            pltpu.VMEM((2, LANES), jnp.int32),
            pltpu.VMEM((1, 2), jnp.int32),
            pltpu.VMEM((CHANS, 2, LANES), BF16),
            pltpu.SemaphoreType.DMA((5,)),
        ],
    )(feats, counts, window_ids.T, occupancy.T, cotangent)
    partner = lax.ppermute(mine, "zh", swap)
    from_core = lax.ppermute(to_core, "c", swap)
    from_chip = lax.ppermute(to_chip, SECTOR, chips)
    loads = pl.pallas_call(
        load_kernel,
        out_shape=struct((16, 96, LANES), BF16),
        in_specs=[hbm, hbm, vmem, vmem, vmem],
        scratch_shapes=[
            pltpu.VMEM(packed, BF16),
            pltpu.VMEM(packed, BF16),
            pltpu.SemaphoreType.DMA((2,)),
        ],
        compiler_params=params,
    )(mine, partner, cot, from_core, from_chip)
    loads = exchange(loads, FACE)
    turned_weight = conv_weight.reshape(3, 9 * CHANS, CHANS).transpose(0, 2, 1)

    blocks = pl.pallas_call(
        ray_kernel,
        out_shape=struct((plane, 112, LANES), BF16),
        in_specs=[vmem, hbm, hbm, vmem],
        scratch_shapes=[
            pltpu.VMEM((3 * CHANS, CHANS), BF16),
            pltpu.VMEM((CHANS, CHANS), BF16),
            pltpu.VMEM((9 * CHANS, 2 * LANES), BF16),
            pltpu.SemaphoreType.DMA((2,)),
        ],
        compiler_params=params,
    )(loads, w_qkv, w_out, turned_weight)
    blocks = exchange(blocks, PLANE)

    terms = whole(sum_kernel, struct((along, 64, LANES), BF16), blocks)
    terms, blocks, partner = lax.optimization_barrier((terms, blocks, partner))
    terms = whole(sum_kernel, struct((plane, 64, LANES), BF16), exchange(terms, RING))

    far = lax.ppermute(partner[2 * CHANS + 16 :], FACE, [(0, face - 1), (face - 1, 0)])
    from_core = lax.ppermute(far, "c", swap)
    edge = lax.dynamic_slice(
        blocks.reshape(face, 2, 112, LANES), (12 * core, core, 64, 0), (4, 1, 32, LANES)
    ).reshape(LANES, LANES)
    halo = lax.ppermute(jnp.concatenate([edge, far], axis=0), SECTOR, chips)
    out, back = pl.pallas_call(
        conv_kernel,
        out_shape=(struct((2, CHANS, LANES), BF16),) * 2,
        in_specs=[vmem] * 6,
        scratch_shapes=[pltpu.VMEM((9 * CHANS, LANES), BF16)],
        compiler_params=params,
    )(blocks, halo, far, from_core, conv_weight, turned_weight)
    out, back = out.transpose(1, 0, 2), back.transpose(1, 0, 2)

    terms, out, back = lax.optimization_barrier((terms, out, back))
    grad_weight = whole(
        unpack_kernel,
        struct((TAPS, CHANS, CHANS), F32),
        exchange(terms, PLANE).reshape(2048, LANES),
    )
    return (out, grad_weight, back)


def solution(mesh):
    mesh = Mesh(mesh.devices.reshape(2, 4, 4, 8, 2), BAND + SECTOR)
    in_specs = (
        P(None, BAND, SECTOR),
        P(BAND, SECTOR),
        P(BAND, SECTOR),
        P(SECTOR, BAND),
        P(),
        P(),
        P(),
        P(None, BAND, SECTOR),
    )
    out_specs = (P(None, BAND, SECTOR), P(), P(None, BAND, SECTOR))
    return jax.shard_map(shards, mesh=mesh, in_specs=in_specs, out_specs=out_specs, check_vma=False)
```

```python
import jax
import jax.numpy as jnp
from jax import lax
from jax.experimental import pallas as pl
from jax.experimental.pallas import tpu as pltpu
from jax.sharding import Mesh
from jax.sharding import PartitionSpec as P

BF16 = jnp.bfloat16
F32 = jnp.float32
CHANS = 96
HEADS = 6
HEAD_DIM = 16
INC = 32
LANES = 128
TAPS = 27
BAND = ("zh", "y", "x")
SECTOR = ("zl", "c")
FACE = ("y", "x")
PLANE = ("y", "x", "c")
RING = ("zh", "zl")


def whole(kernel, outs, *args):
    return pl.pallas_call(
        kernel,
        out_shape=outs,
        compiler_params=pltpu.CompilerParams(vmem_limit_bytes=32 * 1024 * 1024),
    )(*args)


def dot(a, b):
    return jnp.dot(a, b, preferred_element_type=F32)


def iota(shape, dim):
    return lax.broadcasted_iota(jnp.int32, shape, dim)


def lower_half():
    return lax.axis_index("zh") == 0


def first_core():
    return lax.axis_index("c") == 0


def pack_kernel(
    feats_hbm, counts_hbm, ids_hbm, occupancy_hbm, cot_hbm,
    out, turned, to_core, to_chip, feats, counts, ids, occupancy, cot, sems,
):
    pairs = [
        (feats_hbm, feats),
        (counts_hbm, counts),
        (ids_hbm, ids),
        (occupancy_hbm, occupancy),
        (cot_hbm, cot),
    ]
    copies = [pltpu.make_async_copy(*pair, sems.at[i]) for i, pair in enumerate(pairs)]
    for copy in copies:
        copy.start()
    for copy in copies:
        copy.wait()
    both, each = feats[...].astype(F32), cot[...].astype(F32)
    more = []
    for row in range(2):
        out[pl.ds(row * CHANS, CHANS), :] = both[:, row, :].astype(BF16)
        cells = each[:, row, :].astype(BF16)
        turned[row] = cells
        head, tail = each[:, row, :INC], each[:, row, LANES - INC :]
        to_core[row] = jnp.where(first_core(), tail, head).astype(BF16)
        to_chip[row] = jnp.where(first_core(), head, tail).astype(BF16)
        number = ids[row : row + 1, :]
        tag = jnp.where(occupancy[:, row : row + 1] == 1, number, -1)
        more += [v.astype(F32) for v in (counts[row : row + 1, :], number, tag)]
        more.append(jnp.zeros((5, LANES), F32))
    out[pl.ds(2 * CHANS, 16), :] = jnp.concatenate(more, axis=0).astype(BF16)
    edge = jnp.where(lower_half(), each[:, 1, :], each[:, 0, :])
    out[pl.ds(2 * CHANS + 16, CHANS), :] = edge.astype(BF16)


def ray_kernel(loads, w_qkv_hbm, w_out_hbm, turned_weight, out, send, w_qkv, w_out, patches, terms, sems):
    n, wide = 256, 384
    fetches = [
        pltpu.make_async_copy(w_qkv_hbm, w_qkv, sems.at[0]),
        pltpu.make_async_copy(w_out_hbm, w_out, sems.at[1]),
    ]
    for fetch in fetches:
        fetch.start()
    every = loads[...].astype(F32)
    own = every[:, :16].reshape(n, LANES)
    other = every[:, 16:32].reshape(n, LANES)
    low = lower_half()
    edge = jnp.where(low, other[:8], other[n - 8 :])
    asked = jnp.concatenate([own, edge, jnp.zeros((wide - n - 8, LANES), F32)], axis=0)

    def prepared(cells):
        turned = cells.T
        scaled = turned[:CHANS] * jnp.log(2.0 + turned[CHANS : CHANS + 1])
        square = jnp.sum(scaled * scaled, axis=0, keepdims=True) * (1.0 / CHANS)
        return turned, scaled, (scaled * lax.rsqrt(square + 1e-05)).astype(BF16)

    turned, scaled, normed_a = prepared(asked)
    _, _, normed_b = prepared(other)
    for fetch in fetches:
        fetch.wait()
    query = dot(w_qkv[:CHANS, :], normed_a).astype(BF16).astype(F32) * 0.25
    kv = dot(w_qkv[CHANS:, :], jnp.concatenate([normed_a[:, :n], normed_b], axis=1))
    key = kv[:CHANS].T.astype(BF16)
    value = kv[CHANS:].astype(BF16)

    number = turned[CHANS + 1 : CHANS + 2].astype(jnp.int32)
    wanted = (iota((1, wide), 1) % 8) * 4 + number
    wanted = (iota((32, wide), 0) == wanted).astype(F32).astype(BF16)
    tag = jnp.concatenate(
        [own[:, CHANS + 2 : CHANS + 3], other[:, CHANS + 2 : CHANS + 3]], axis=0
    ).astype(jnp.int32)
    given = jnp.where(tag < 0, -1, (iota((2 * n, 1), 0) % 8) * 4 + tag)
    given = (iota((2 * n, 32), 1) == given).astype(F32).astype(BF16)
    place = iota((1, wide), 1)
    place = jnp.where((place < n) | low, place, place + n - 8)
    allowed = (dot(given, wanted) > 0.5) | (iota((2 * n, wide), 0) == place)
    bias = jnp.where(allowed, 0.0, -1e30)

    cell = iota((16, 8, LANES), 1)
    for da in range(3):
        shifted = [[], [], []]
        for row in range(2):
            at, edge_at = 32 + da * 16 + row * 8, 80 + da * 4 + row * 2
            block = every[:, at : at + 8]
            flat = block.reshape(LANES, LANES)
            upper = pltpu.roll(flat, LANES - 1, 0).reshape(16, 8, LANES)
            lower = pltpu.roll(flat, 1, 0).reshape(16, 8, LANES)
            shifted[0].append(jnp.where(cell < 7, upper, every[:, edge_at + 1 : edge_at + 2]))
            shifted[1].append(block)
            shifted[2].append(jnp.where(cell > 0, lower, every[:, edge_at : edge_at + 1]))
        for di in range(3):
            cells = jnp.concatenate(shifted[di], axis=1).reshape(n, LANES)
            patches[pl.ds((da * 3 + di) * CHANS, CHANS), :] = cells.T[:CHANS].astype(BF16)

    channel = iota((CHANS, wide), 0) // HEAD_DIM
    heads = []
    for head in range(HEADS):
        mine = jnp.where(channel == head, query, 0.0).astype(BF16)
        score = dot(key, mine) + bias
        weight = jnp.exp(score - jnp.max(score, axis=0, keepdims=True))
        total = jnp.sum(weight, axis=0, keepdims=True)
        summed = dot(value[head * HEAD_DIM : (head + 1) * HEAD_DIM], weight.astype(BF16))
        heads.append((summed / total).astype(BF16))
    attn = jnp.concatenate(heads, axis=0)
    mid = scaled + dot(w_out[...], attn)
    mid = jnp.concatenate([mid, jnp.zeros((LANES - CHANS, wide), F32)], axis=0).T
    edge, none = mid[n : n + 8], jnp.zeros((8, LANES), F32)
    mid = jnp.concatenate(
        [jnp.where(low, none, edge), mid[:n], jnp.where(low, edge, none)], axis=0
    )
    pairs = mid.reshape(17, 16, LANES)
    pairs = jnp.concatenate([pairs[:16], pairs[1:]], axis=1).astype(BF16)

    near = [mid[8 * dr : 8 * dr + n].astype(BF16) for dr in range(3)]
    lane = iota((CHANS, LANES), 1)
    for group in range(7):
        parts = [
            dot(patches[pl.ds(tap % 9 * CHANS, CHANS), :], near[tap // 9])
            for tap in range(group * 4, min(group * 4 + 4, TAPS))
        ]
        for j in range(3):
            tile = parts[j]
            if len(parts) == 4:
                tile = jnp.where(lane < CHANS, tile, pltpu.roll(parts[3], 96 - 32 * j, 1))
            tile = tile.astype(BF16)
            for q in range(3):
                at = (group * 3 + j) * CHANS + 32 * q
                core, face = at // 64 % 2, at // 128
                terms[core, face, pl.ds(at % 64, 32), :] = tile[32 * q : 32 * q + 32]
    terms[1, 15, pl.ds(32, 32), :] = jnp.zeros((32, LANES), BF16)
    core = lax.axis_index("c")
    out[:, pl.ds(0, 64), :] = terms[core]
    send[...] = terms[1 - core]

    lane = iota((CHANS, n), 1)
    up, level, down = (dot(turned_weight[dr], patches[...]) for dr in range(3))
    back = level + jnp.where(lane < n - 8, pltpu.roll(up, n - 8, 1), 0.0)
    back = back + jnp.where(lane >= 8, pltpu.roll(down, 8, 1), 0.0)
    back = jnp.concatenate([back, jnp.zeros((LANES - CHANS, n), F32)], axis=0).T
    out[:, pl.ds(64, 32), :] = pairs
    out[:, pl.ds(96, 16), :] = back.astype(BF16).reshape(16, 16, LANES)


def join_kernel(blocks, got, out):
    total = blocks[:, pl.ds(0, 64), :].astype(F32) + got[...].astype(F32)
    out[:, pl.ds(0, 64), :] = total.astype(BF16)
    out[:, pl.ds(64, 48), :] = blocks[:, pl.ds(64, 48), :]


def moves():
    source, target = iota((6 * INC, LANES), 0), iota((6 * INC, LANES), 1)
    for da in range(3):
        for di in range(3):
            at = target % INC + 1 - di
            move = (source == target + (2 - da) * INC + 1 - di) & (at >= 0) & (at < INC)
            yield da, di, move.astype(F32).astype(BF16)


def as_voxels(packed):
    voxels = []
    for row in range(2):
        parts = [
            packed[pl.ds(row * CHANS, CHANS), :].astype(F32),
            packed[pl.ds(2 * CHANS, 16), :].astype(F32)[row * 8 : row * 8 + 8],
            jnp.zeros((LANES - CHANS - 8, LANES), F32),
        ]
        voxels.append(jnp.concatenate(parts, axis=0).T.reshape(16, 8, LANES))
    return jnp.concatenate(voxels, axis=1).astype(BF16)


def partner_kernel(partner_hbm, loads_hbm, out_hbm, partner, voxels, sem):
    del loads_hbm
    fetch = pltpu.make_async_copy(partner_hbm, partner, sem)
    fetch.start()
    fetch.wait()
    voxels[...] = as_voxels(partner)
    put = pltpu.make_async_copy(voxels, out_hbm.at[:, pl.ds(16, 16), :], sem)
    put.start()
    put.wait()


def load_kernel(mine, middle, from_core, from_chip, out):
    inc = iota((6 * INC, LANES), 0) % INC
    rows = []
    for row in range(2):
        parts = []
        core, chip = from_core[row].astype(F32), from_chip[row].astype(F32)
        left, right = jnp.where(first_core(), chip, core), jnp.where(first_core(), core, chip)
        for cells in (left, middle[row].astype(F32), right):
            more = jnp.zeros((LANES - CHANS, cells.shape[1]), F32)
            parts.append(jnp.concatenate([cells, more], axis=0).T)
        cells = jnp.concatenate(parts, axis=0)
        lower = jnp.where(inc > 0, pltpu.roll(cells, 1, 0), 0.0)
        upper = jnp.where(inc < INC - 1, pltpu.roll(cells, 6 * INC - 1, 0), 0.0)
        rows.append((cells, lower, upper))
    blocks, edges = [], []
    for da in range(3):
        at = (2 - da) * INC
        for row in range(2):
            cells, lower, upper = (v[at : at + LANES].reshape(16, 8, LANES) for v in rows[row])
            blocks.append(cells)
            edges += [lower[:, :1], upper[:, 7:]]
    edges.append(jnp.zeros((16, 4, LANES), F32))
    out[:, pl.ds(0, 16), :] = as_voxels(mine)
    out[:, pl.ds(16, 16), :] = jnp.zeros((16, 16, LANES), BF16)
    out[:, pl.ds(32, 48), :] = jnp.concatenate(blocks, axis=1).astype(BF16)
    out[:, pl.ds(80, 16), :] = jnp.concatenate(edges, axis=1).astype(BF16)


def by_rows(cells):
    cells = cells.astype(F32)
    return [cells[:, r * 8 : r * 8 + 8, :].reshape(-1, LANES) for r in range(cells.shape[1] // 8)]


def sum_kernel(terms, out):
    total = jnp.sum(terms[:, pl.ds(0, 64), :].astype(F32), axis=0, keepdims=True)
    out[...] = jnp.broadcast_to(total, out.shape).astype(BF16)


def unpack_kernel(tiles, out):
    lane = iota((CHANS, LANES), 1)
    for group in range(7):
        parts = [
            tiles[pl.ds((group * 3 + j) * CHANS, CHANS), :].astype(F32) for j in range(3)
        ]
        for j in range(3):
            out[group * 4 + j] = parts[j][:, :CHANS]
        if group * 4 + 3 < TAPS:
            turned = [pltpu.roll(parts[j], 32 + 32 * j, 1) for j in range(3)]
            last = jnp.where(lane < 32, turned[0], jnp.where(lane < 64, turned[1], turned[2]))
            out[group * 4 + 3] = last[:, :CHANS]


def conv_kernel(blocks, from_chip, far, from_core, weight, turned_weight, out, back, patches):
    low, first = lower_half(), first_core()
    mine = blocks[:, pl.ds(64, 48), :].astype(F32)
    core, chip = from_core[...].astype(F32), from_chip[...].astype(F32)
    left, right = jnp.where(first, chip, core), jnp.where(first, core, chip)
    before, after = left[LANES:], right[LANES:]
    left, right = left[:LANES].reshape(4, 32, LANES), right[:LANES].reshape(4, 32, LANES)
    beyond = [before[:, LANES - INC :], far[...].astype(F32), after[:, :INC]]
    at = lax.axis_index("y") * lax.axis_size("x") + lax.axis_index("x")
    reached = at == jnp.where(low, 15, 0)
    beyond = jnp.where(reached, jnp.concatenate(beyond, axis=1), 0.0).astype(BF16)
    for da, di, move in moves():
        patches[pl.ds((da * 3 + di) * CHANS, CHANS), :] = dot(beyond, move).astype(BF16)
    more = [dot(turned_weight[dr], patches[...]) for dr in (2, 0)]
    more = [jnp.where(low, 0.0, more[0]), jnp.where(low, more[1], 0.0)]
    for row, cells in enumerate(by_rows(mine[:, 32:])):
        back[row] = (cells.T[:CHANS] + more[row]).astype(BF16)

    rows = by_rows(jnp.concatenate([left, mine[:, :32], right], axis=0))
    inc = iota((6 * INC, LANES), 0) % INC
    moved = []
    for row in rows:
        moved.append(
            [
                jnp.where(inc > 0, pltpu.roll(row, 1, 0), 0.0).astype(BF16),
                row.astype(BF16),
                jnp.where(inc < INC - 1, pltpu.roll(row, 6 * INC - 1, 0), 0.0).astype(BF16),
            ]
        )
    for row in range(2):
        total = jnp.zeros((LANES, CHANS), F32)
        for tap in range(TAPS):
            dr, da, di = tap // 9, tap // 3 % 3, tap % 3
            patch = moved[row + dr][di][da * INC : da * INC + LANES, :CHANS]
            total = total + lax.dot_general(
                patch, weight[tap], (((1,), (1,)), ((), ())), preferred_element_type=F32
            )
        out[row] = total.T.astype(BF16)


def exchange(cells, axis):
    return lax.all_to_all(cells, axis, 0, 0, tiled=True)


def shards(feats, counts, occupancy, window_ids, w_qkv, w_out, conv_weight, cotangent):
    struct = jax.ShapeDtypeStruct
    sectors = lax.axis_size(SECTOR)
    core = lax.axis_index("c")
    plane, along, face = lax.axis_size(PLANE), lax.axis_size(RING), lax.axis_size(FACE)
    vmem, hbm = pl.BlockSpec(memory_space=pltpu.VMEM), pl.BlockSpec(memory_space=pl.ANY)
    params = pltpu.CompilerParams(vmem_limit_bytes=32 * 1024 * 1024)
    chips = [(i, (i + 1) % sectors) for i in range(1, sectors, 2)]
    chips += [(j, i) for i, j in chips]
    swap = [(0, 1), (1, 0)]
    packed, edge = (3 * CHANS + 16, LANES), struct((2, CHANS, INC), BF16)
    mine, cot, to_core, to_chip = pl.pallas_call(
        pack_kernel,
        out_shape=(struct(packed, BF16), struct((2, CHANS, LANES), BF16), edge, edge),
        in_specs=[hbm] * 5,
        scratch_shapes=[
            pltpu.VMEM((CHANS, 2, LANES), BF16),
            pltpu.VMEM((2, LANES), jnp.int32),
            pltpu.VMEM((2, LANES), jnp.int32),
            pltpu.VMEM((1, 2), jnp.int32),
            pltpu.VMEM((CHANS, 2, LANES), BF16),
            pltpu.SemaphoreType.DMA((5,)),
        ],
    )(feats, counts, window_ids.T, occupancy.T, cotangent)
    partner = lax.ppermute(mine, "zh", swap)
    from_core = lax.ppermute(to_core, "c", swap)
    from_chip = lax.ppermute(to_chip, SECTOR, chips)
    loads = whole(load_kernel, struct((16, 96, LANES), BF16), mine, cot, from_core, from_chip)
    loads = pl.pallas_call(
        partner_kernel,
        out_shape=struct((16, 96, LANES), BF16),
        in_specs=[hbm, hbm],
        out_specs=hbm,
        scratch_shapes=[
            pltpu.VMEM(packed, BF16),
            pltpu.VMEM((16, 16, LANES), BF16),
            pltpu.SemaphoreType.DMA,
        ],
        input_output_aliases={1: 0},
        compiler_params=params,
    )(partner, loads)
    loads = exchange(loads, FACE)
    turned_weight = conv_weight.reshape(3, 9 * CHANS, CHANS).transpose(0, 2, 1)

    blocks, send = pl.pallas_call(
        ray_kernel,
        out_shape=(struct((face, 112, LANES), BF16), struct((face, 64, LANES), BF16)),
        in_specs=[vmem, hbm, hbm, vmem],
        scratch_shapes=[
            pltpu.VMEM((3 * CHANS, CHANS), BF16),
            pltpu.VMEM((CHANS, CHANS), BF16),
            pltpu.VMEM((9 * CHANS, 2 * LANES), BF16),
            pltpu.VMEM((2, face, 64, LANES), BF16),
            pltpu.SemaphoreType.DMA((2,)),
        ],
        compiler_params=params,
    )(loads, w_qkv, w_out, turned_weight)
    got = lax.ppermute(send, "c", swap)
    blocks = exchange(whole(join_kernel, struct((face, 112, LANES), BF16), blocks, got), FACE)

    terms = whole(sum_kernel, struct((along, 64, LANES), BF16), blocks)
    terms, blocks, partner = lax.optimization_barrier((terms, blocks, partner))
    terms = whole(sum_kernel, struct((plane, 64, LANES), BF16), exchange(terms, RING))

    far = lax.ppermute(partner[2 * CHANS + 16 :], FACE, [(0, face - 1), (face - 1, 0)])

    def edge_of(start):
        piece = lax.dynamic_slice(blocks, (start, 64, 0), (4, 32, LANES))
        return jnp.concatenate([piece.reshape(LANES, LANES), far], axis=0)

    from_chip = lax.ppermute(edge_of(12 * core), SECTOR, chips)
    from_core = lax.ppermute(edge_of(12 * (1 - core)), "c", swap)
    out, back = pl.pallas_call(
        conv_kernel,
        out_shape=(struct((2, CHANS, LANES), BF16),) * 2,
        in_specs=[vmem] * 6,
        scratch_shapes=[pltpu.VMEM((9 * CHANS, LANES), BF16)],
        compiler_params=params,
        cost_estimate=pl.CostEstimate(flops=10**11, bytes_accessed=2**21, transcendentals=0),
    )(blocks, from_chip, far, from_core, conv_weight, turned_weight)
    out, back = out.transpose(1, 0, 2), back.transpose(1, 0, 2)

    grad_weight = whole(
        unpack_kernel,
        struct((TAPS, CHANS, CHANS), F32),
        exchange(terms, PLANE).reshape(2048, LANES),
    )
    return (out, grad_weight, back)


def solution(mesh):
    mesh = Mesh(mesh.devices.reshape(2, 4, 4, 8, 2), BAND + SECTOR)
    in_specs = (
        P(None, BAND, SECTOR),
        P(BAND, SECTOR),
        P(BAND, SECTOR),
        P(SECTOR, BAND),
        P(),
        P(),
        P(),
        P(None, BAND, SECTOR),
    )
    out_specs = (P(None, BAND, SECTOR), P(), P(None, BAND, SECTOR))
    return jax.shard_map(shards, mesh=mesh, in_specs=in_specs, out_specs=out_specs, check_vma=False)
```

```python
import jax
import jax.numpy as jnp
from jax import lax
from jax.experimental import pallas as pl
from jax.experimental.pallas import tpu as pltpu
from jax.sharding import Mesh
from jax.sharding import PartitionSpec as P

BF16 = jnp.bfloat16
F32 = jnp.float32
CHANS = 96
HEADS = 6
HEAD_DIM = 16
INC = 32
LANES = 128
TAPS = 27
BAND = ("zh", "y", "x")
SECTOR = ("zl", "c")
FACE = ("y", "x")
PLANE = ("y", "x", "c")
RING = ("zh", "zl")


def whole(kernel, outs, *args):
    return pl.pallas_call(
        kernel,
        out_shape=outs,
        compiler_params=pltpu.CompilerParams(vmem_limit_bytes=32 * 1024 * 1024),
    )(*args)


def dot(a, b):
    return jnp.dot(a, b, preferred_element_type=F32)


def iota(shape, dim):
    return lax.broadcasted_iota(jnp.int32, shape, dim)


def lower_half():
    return lax.axis_index("zh") == 0


def first_core():
    return lax.axis_index("c") == 0


def pack_kernel(
    feats_hbm, counts_hbm, ids_hbm, occupancy_hbm, cot_hbm,
    out, turned, to_core, to_chip, feats, counts, ids, occupancy, cot, sems,
):
    pairs = [
        (feats_hbm, feats),
        (counts_hbm, counts),
        (ids_hbm, ids),
        (occupancy_hbm, occupancy),
        (cot_hbm, cot),
    ]
    copies = [pltpu.make_async_copy(*pair, sems.at[i]) for i, pair in enumerate(pairs)]
    for copy in copies:
        copy.start()
    for copy in copies:
        copy.wait()
    both, each = feats[...].astype(F32), cot[...].astype(F32)
    more = []
    for row in range(2):
        out[pl.ds(row * CHANS, CHANS), :] = both[:, row, :].astype(BF16)
        cells = each[:, row, :].astype(BF16)
        turned[row] = cells
        head, tail = each[:, row, :INC], each[:, row, LANES - INC :]
        to_core[row] = jnp.where(first_core(), tail, head).astype(BF16)
        to_chip[row] = jnp.where(first_core(), head, tail).astype(BF16)
        number = ids[row : row + 1, :]
        tag = jnp.where(occupancy[:, row : row + 1] == 1, number, -1)
        more += [v.astype(F32) for v in (counts[row : row + 1, :], number, tag)]
        more.append(jnp.zeros((5, LANES), F32))
    out[pl.ds(2 * CHANS, 16), :] = jnp.concatenate(more, axis=0).astype(BF16)
    edge = jnp.where(lower_half(), each[:, 1, :], each[:, 0, :])
    out[pl.ds(2 * CHANS + 16, CHANS), :] = edge.astype(BF16)


def ray_kernel(loads, w_qkv_hbm, w_out_hbm, turned_weight, out, send, w_qkv, w_out, patches, terms, sems):
    n, wide = 256, 384
    fetches = [
        pltpu.make_async_copy(w_qkv_hbm, w_qkv, sems.at[0]),
        pltpu.make_async_copy(w_out_hbm, w_out, sems.at[1]),
    ]
    for fetch in fetches:
        fetch.start()
    every = loads[...].astype(F32)
    own = every[:, :16].reshape(n, LANES)
    other = every[:, 16:32].reshape(n, LANES)
    low = lower_half()
    edge = jnp.where(low, other[:8], other[n - 8 :])
    asked = jnp.concatenate([own, edge, jnp.zeros((wide - n - 8, LANES), F32)], axis=0)

    def prepared(cells):
        turned = cells.T
        scaled = turned[:CHANS] * jnp.log(2.0 + turned[CHANS : CHANS + 1])
        square = jnp.sum(scaled * scaled, axis=0, keepdims=True) * (1.0 / CHANS)
        return turned, scaled, (scaled * lax.rsqrt(square + 1e-05)).astype(BF16)

    turned, scaled, normed_a = prepared(asked)
    _, _, normed_b = prepared(other)
    for fetch in fetches:
        fetch.wait()
    query = dot(w_qkv[:CHANS, :], normed_a).astype(BF16).astype(F32) * 0.25
    kv = dot(w_qkv[CHANS:, :], jnp.concatenate([normed_a[:, :n], normed_b], axis=1))
    key = kv[:CHANS].T.astype(BF16)
    value = kv[CHANS:].astype(BF16)

    number = turned[CHANS + 1 : CHANS + 2].astype(jnp.int32)
    wanted = (iota((1, wide), 1) % 8) * 4 + number
    wanted = (iota((32, wide), 0) == wanted).astype(F32).astype(BF16)
    tag = jnp.concatenate(
        [own[:, CHANS + 2 : CHANS + 3], other[:, CHANS + 2 : CHANS + 3]], axis=0
    ).astype(jnp.int32)
    given = jnp.where(tag < 0, -1, (iota((2 * n, 1), 0) % 8) * 4 + tag)
    given = (iota((2 * n, 32), 1) == given).astype(F32).astype(BF16)
    place = iota((1, wide), 1)
    place = jnp.where((place < n) | low, place, place + n - 8)
    allowed = (dot(given, wanted) > 0.5) | (iota((2 * n, wide), 0) == place)
    bias = jnp.where(allowed, 0.0, -1e30)

    cell = iota((16, 8, LANES), 1)
    for da in range(3):
        shifted = [[], [], []]
        for row in range(2):
            at, edge_at = 32 + da * 16 + row * 8, 80 + da * 4 + row * 2
            block = every[:, at : at + 8]
            flat = block.reshape(LANES, LANES)
            upper = pltpu.roll(flat, LANES - 1, 0).reshape(16, 8, LANES)
            lower = pltpu.roll(flat, 1, 0).reshape(16, 8, LANES)
            shifted[0].append(jnp.where(cell < 7, upper, every[:, edge_at + 1 : edge_at + 2]))
            shifted[1].append(block)
            shifted[2].append(jnp.where(cell > 0, lower, every[:, edge_at : edge_at + 1]))
        for di in range(3):
            cells = jnp.concatenate(shifted[di], axis=1).reshape(n, LANES)
            patches[pl.ds((da * 3 + di) * CHANS, CHANS), :] = cells.T[:CHANS].astype(BF16)

    channel = iota((CHANS, wide), 0) // HEAD_DIM
    heads = []
    for head in range(HEADS):
        mine = jnp.where(channel == head, query, 0.0).astype(BF16)
        score = dot(key, mine) + bias
        weight = jnp.exp(score - jnp.max(score, axis=0, keepdims=True))
        total = jnp.sum(weight, axis=0, keepdims=True)
        summed = dot(value[head * HEAD_DIM : (head + 1) * HEAD_DIM], weight.astype(BF16))
        heads.append((summed / total).astype(BF16))
    attn = jnp.concatenate(heads, axis=0)
    mid = scaled + dot(w_out[...], attn)
    mid = jnp.concatenate([mid, jnp.zeros((LANES - CHANS, wide), F32)], axis=0).T
    edge, none = mid[n : n + 8], jnp.zeros((8, LANES), F32)
    mid = jnp.concatenate(
        [jnp.where(low, none, edge), mid[:n], jnp.where(low, edge, none)], axis=0
    )
    pairs = mid.reshape(17, 16, LANES)
    pairs = jnp.concatenate([pairs[:16], pairs[1:]], axis=1).astype(BF16)

    near = [mid[8 * dr : 8 * dr + n].astype(BF16) for dr in range(3)]
    lane = iota((CHANS, LANES), 1)
    for group in range(7):
        parts = [
            dot(patches[pl.ds(tap % 9 * CHANS, CHANS), :], near[tap // 9])
            for tap in range(group * 4, min(group * 4 + 4, TAPS))
        ]
        for j in range(3):
            tile = parts[j]
            if len(parts) == 4:
                tile = jnp.where(lane < CHANS, tile, pltpu.roll(parts[3], 96 - 32 * j, 1))
            tile = tile.astype(BF16)
            for q in range(3):
                at = (group * 3 + j) * CHANS + 32 * q
                core, face = at // 64 % 2, at // 128
                terms[core, face, pl.ds(at % 64, 32), :] = tile[32 * q : 32 * q + 32]
    terms[1, 15, pl.ds(32, 32), :] = jnp.zeros((32, LANES), BF16)
    core = lax.axis_index("c")
    out[:, pl.ds(0, 64), :] = terms[core]
    send[...] = terms[1 - core]

    lane = iota((CHANS, n), 1)
    up, level, down = (dot(turned_weight[dr], patches[...]) for dr in range(3))
    back = level + jnp.where(lane < n - 8, pltpu.roll(up, n - 8, 1), 0.0)
    back = back + jnp.where(lane >= 8, pltpu.roll(down, 8, 1), 0.0)
    back = jnp.concatenate([back, jnp.zeros((LANES - CHANS, n), F32)], axis=0).T
    out[:, pl.ds(64, 32), :] = pairs
    out[:, pl.ds(96, 16), :] = back.astype(BF16).reshape(16, 16, LANES)


def join_kernel(blocks, got, out):
    total = blocks[:, pl.ds(0, 64), :].astype(F32) + got[...].astype(F32)
    out[:, pl.ds(0, 64), :] = total.astype(BF16)
    out[:, pl.ds(64, 48), :] = blocks[:, pl.ds(64, 48), :]


def moves():
    source, target = iota((6 * INC, LANES), 0), iota((6 * INC, LANES), 1)
    for da in range(3):
        for di in range(3):
            at = target % INC + 1 - di
            move = (source == target + (2 - da) * INC + 1 - di) & (at >= 0) & (at < INC)
            yield da, di, move.astype(F32).astype(BF16)


def as_voxels(packed):
    voxels = []
    for row in range(2):
        parts = [
            packed[pl.ds(row * CHANS, CHANS), :].astype(F32),
            packed[pl.ds(2 * CHANS, 16), :].astype(F32)[row * 8 : row * 8 + 8],
            jnp.zeros((LANES - CHANS - 8, LANES), F32),
        ]
        voxels.append(jnp.concatenate(parts, axis=0).T.reshape(16, 8, LANES))
    return jnp.concatenate(voxels, axis=1).astype(BF16)


def partner_kernel(partner_hbm, loads_hbm, out_hbm, partner, voxels, sem):
    del loads_hbm
    fetch = pltpu.make_async_copy(partner_hbm, partner, sem)
    fetch.start()
    fetch.wait()
    voxels[...] = as_voxels(partner)
    put = pltpu.make_async_copy(voxels, out_hbm.at[:, pl.ds(16, 16), :], sem)
    put.start()
    put.wait()


def load_kernel(mine, middle, from_core, from_chip, out):
    inc = iota((6 * INC, LANES), 0) % INC
    rows = []
    for row in range(2):
        parts = []
        core, chip = from_core[row].astype(F32), from_chip[row].astype(F32)
        left, right = jnp.where(first_core(), chip, core), jnp.where(first_core(), core, chip)
        for cells in (left, middle[row].astype(F32), right):
            more = jnp.zeros((LANES - CHANS, cells.shape[1]), F32)
            parts.append(jnp.concatenate([cells, more], axis=0).T)
        cells = jnp.concatenate(parts, axis=0)
        lower = jnp.where(inc > 0, pltpu.roll(cells, 1, 0), 0.0)
        upper = jnp.where(inc < INC - 1, pltpu.roll(cells, 6 * INC - 1, 0), 0.0)
        rows.append((cells, lower, upper))
    blocks, edges = [], []
    for da in range(3):
        at = (2 - da) * INC
        for row in range(2):
            cells, lower, upper = (v[at : at + LANES].reshape(16, 8, LANES) for v in rows[row])
            blocks.append(cells)
            edges += [lower[:, :1], upper[:, 7:]]
    edges.append(jnp.zeros((16, 4, LANES), F32))
    out[:, pl.ds(0, 16), :] = as_voxels(mine)
    out[:, pl.ds(16, 16), :] = jnp.zeros((16, 16, LANES), BF16)
    out[:, pl.ds(32, 48), :] = jnp.concatenate(blocks, axis=1).astype(BF16)
    out[:, pl.ds(80, 16), :] = jnp.concatenate(edges, axis=1).astype(BF16)


def by_rows(cells):
    cells = cells.astype(F32)
    return [cells[:, r * 8 : r * 8 + 8, :].reshape(-1, LANES) for r in range(cells.shape[1] // 8)]


def sum_kernel(terms, out):
    total = jnp.sum(terms[:, pl.ds(0, 64), :].astype(F32), axis=0, keepdims=True)
    out[...] = jnp.broadcast_to(total, out.shape).astype(BF16)


def unpack_kernel(tiles, out):
    lane = iota((CHANS, LANES), 1)
    for group in range(7):
        parts = [
            tiles[pl.ds((group * 3 + j) * CHANS, CHANS), :].astype(F32) for j in range(3)
        ]
        for j in range(3):
            out[group * 4 + j] = parts[j][:, :CHANS]
        if group * 4 + 3 < TAPS:
            turned = [pltpu.roll(parts[j], 32 + 32 * j, 1) for j in range(3)]
            last = jnp.where(lane < 32, turned[0], jnp.where(lane < 64, turned[1], turned[2]))
            out[group * 4 + 3] = last[:, :CHANS]


def conv_kernel(blocks, from_core, far, from_chip, weight, turned_weight, out, back, patches):
    low, first = lower_half(), first_core()
    mine = blocks[:, pl.ds(64, 48), :].astype(F32)
    core, chip = from_core[...].astype(F32), from_chip[...].astype(F32)
    left, right = jnp.where(first, chip, core), jnp.where(first, core, chip)
    before, after = left[LANES:], right[LANES:]
    left, right = left[:LANES].reshape(4, 32, LANES), right[:LANES].reshape(4, 32, LANES)
    beyond = [before[:, LANES - INC :], far[...].astype(F32), after[:, :INC]]
    at = lax.axis_index("y") * lax.axis_size("x") + lax.axis_index("x")
    reached = at == jnp.where(low, 15, 0)
    beyond = jnp.where(reached, jnp.concatenate(beyond, axis=1), 0.0).astype(BF16)
    for da, di, move in moves():
        patches[pl.ds((da * 3 + di) * CHANS, CHANS), :] = dot(beyond, move).astype(BF16)
    more = [dot(turned_weight[dr], patches[...]) for dr in (2, 0)]
    more = [jnp.where(low, 0.0, more[0]), jnp.where(low, more[1], 0.0)]
    for row, cells in enumerate(by_rows(mine[:, 32:])):
        back[row] = (cells.T[:CHANS] + more[row]).astype(BF16)

    rows = by_rows(jnp.concatenate([left, mine[:, :32], right], axis=0))
    inc = iota((6 * INC, LANES), 0) % INC
    moved = []
    for row in rows:
        moved.append(
            [
                jnp.where(inc > 0, pltpu.roll(row, 1, 0), 0.0).astype(BF16),
                row.astype(BF16),
                jnp.where(inc < INC - 1, pltpu.roll(row, 6 * INC - 1, 0), 0.0).astype(BF16),
            ]
        )
    for row in range(2):
        total = jnp.zeros((LANES, CHANS), F32)
        for tap in range(TAPS):
            dr, da, di = tap // 9, tap // 3 % 3, tap % 3
            patch = moved[row + dr][di][da * INC : da * INC + LANES, :CHANS]
            total = total + lax.dot_general(
                patch, weight[tap], (((1,), (1,)), ((), ())), preferred_element_type=F32
            )
        out[row] = total.T.astype(BF16)


def exchange(cells, axis):
    return lax.all_to_all(cells, axis, 0, 0, tiled=True)


def shards(feats, counts, occupancy, window_ids, w_qkv, w_out, conv_weight, cotangent):
    struct = jax.ShapeDtypeStruct
    sectors = lax.axis_size(SECTOR)
    core = lax.axis_index("c")
    plane, along, face = lax.axis_size(PLANE), lax.axis_size(RING), lax.axis_size(FACE)
    vmem, hbm = pl.BlockSpec(memory_space=pltpu.VMEM), pl.BlockSpec(memory_space=pl.ANY)
    params = pltpu.CompilerParams(vmem_limit_bytes=32 * 1024 * 1024)
    chips = [(i, (i + 1) % sectors) for i in range(1, sectors, 2)]
    chips += [(j, i) for i, j in chips]
    swap = [(0, 1), (1, 0)]
    packed, edge = (3 * CHANS + 16, LANES), struct((2, CHANS, INC), BF16)
    mine, cot, to_core, to_chip = pl.pallas_call(
        pack_kernel,
        out_shape=(struct(packed, BF16), struct((2, CHANS, LANES), BF16), edge, edge),
        in_specs=[hbm] * 5,
        scratch_shapes=[
            pltpu.VMEM((CHANS, 2, LANES), BF16),
            pltpu.VMEM((2, LANES), jnp.int32),
            pltpu.VMEM((2, LANES), jnp.int32),
            pltpu.VMEM((1, 2), jnp.int32),
            pltpu.VMEM((CHANS, 2, LANES), BF16),
            pltpu.SemaphoreType.DMA((5,)),
        ],
    )(feats, counts, window_ids.T, occupancy.T, cotangent)
    partner = lax.ppermute(mine, "zh", swap)
    from_core = lax.ppermute(to_core, "c", swap)
    from_chip = lax.ppermute(to_chip, SECTOR, chips)
    loads = whole(load_kernel, struct((16, 96, LANES), BF16), mine, cot, from_core, from_chip)
    loads = pl.pallas_call(
        partner_kernel,
        out_shape=struct((16, 96, LANES), BF16),
        in_specs=[hbm, hbm],
        out_specs=hbm,
        scratch_shapes=[
            pltpu.VMEM(packed, BF16),
            pltpu.VMEM((16, 16, LANES), BF16),
            pltpu.SemaphoreType.DMA,
        ],
        input_output_aliases={1: 0},
        compiler_params=params,
    )(partner, loads)
    loads = exchange(loads, FACE)
    turned_weight = conv_weight.reshape(3, 9 * CHANS, CHANS).transpose(0, 2, 1)

    blocks, send = pl.pallas_call(
        ray_kernel,
        out_shape=(struct((face, 112, LANES), BF16), struct((face, 64, LANES), BF16)),
        in_specs=[vmem, hbm, hbm, vmem],
        scratch_shapes=[
            pltpu.VMEM((3 * CHANS, CHANS), BF16),
            pltpu.VMEM((CHANS, CHANS), BF16),
            pltpu.VMEM((9 * CHANS, 2 * LANES), BF16),
            pltpu.VMEM((2, face, 64, LANES), BF16),
            pltpu.SemaphoreType.DMA((2,)),
        ],
        compiler_params=params,
    )(loads, w_qkv, w_out, turned_weight)
    got = lax.ppermute(send, "c", swap)
    blocks = exchange(whole(join_kernel, struct((face, 112, LANES), BF16), blocks, got), FACE)

    terms = whole(sum_kernel, struct((along, 64, LANES), BF16), blocks)
    terms, blocks, partner = lax.optimization_barrier((terms, blocks, partner))
    terms = whole(sum_kernel, struct((plane, 64, LANES), BF16), exchange(terms, RING))

    far = lax.ppermute(partner[2 * CHANS + 16 :], FACE, [(0, face - 1), (face - 1, 0)])

    def edge_of(start):
        piece = lax.dynamic_slice(blocks, (start, 64, 0), (4, 32, LANES))
        return jnp.concatenate([piece.reshape(LANES, LANES), far], axis=0)

    from_core = lax.ppermute(edge_of(12 * (1 - core)), "c", swap)
    from_chip = lax.ppermute(edge_of(12 * core), SECTOR, chips)
    out, back = pl.pallas_call(
        conv_kernel,
        out_shape=(struct((2, CHANS, LANES), BF16),) * 2,
        in_specs=[vmem] * 6,
        scratch_shapes=[pltpu.VMEM((9 * CHANS, LANES), BF16)],
        compiler_params=params,
        cost_estimate=pl.CostEstimate(flops=10**11, bytes_accessed=2**21, transcendentals=0),
    )(blocks, from_core, far, from_chip, conv_weight, turned_weight)
    out, back = out.transpose(1, 0, 2), back.transpose(1, 0, 2)

    grad_weight = whole(
        unpack_kernel,
        struct((TAPS, CHANS, CHANS), F32),
        exchange(terms, PLANE).reshape(2048, LANES),
    )
    return (out, grad_weight, back)


def solution(mesh):
    mesh = Mesh(mesh.devices.reshape(2, 4, 4, 8, 2), BAND + SECTOR)
    in_specs = (
        P(None, BAND, SECTOR),
        P(BAND, SECTOR),
        P(BAND, SECTOR),
        P(SECTOR, BAND),
        P(),
        P(),
        P(),
        P(None, BAND, SECTOR),
    )
    out_specs = (P(None, BAND, SECTOR), P(), P(None, BAND, SECTOR))
    return jax.shard_map(shards, mesh=mesh, in_specs=in_specs, out_specs=out_specs, check_vma=False)
```
